256 devices in a mesh: depth: 8 (over y, z_lo), plane: 32 (over x, z_hi, core).
Axes of the slice: x: 4, y: 4, z: 8 (z_hi: 4, z_lo: 2; z = z_hi * 2 + z_lo), core: 2. Of those that a mesh axis runs over, the one named last changes fastest.
Arguments:
- velocity: float32 [24, 2048, 2048], P('depth', 'plane'), may hold values from 1.5 to 6
- dual_field: float32 [3, 24, 2048, 2048], P(None, 'depth', 'plane'), may hold values from -3 to 3
- kernel: float32 [24, 2048, 2048], P('depth', 'plane'), may hold values from 0.5 to 5
- data_spec: float32 [2048, 2048], P('plane'), may hold values from -12 to 12
Outputs:
- velocity_new: float32 [24, 2048, 2048], P('depth', 'plane')
- dual_new: float32 [3, 24, 2048, 2048], P(None, 'depth', 'plane')
The draws below stay inside these ranges and needn't reach their ends.
All inputs are finite; a program needn't handle non-finite values.
Results may differ from the reference program's by a relative error of at most 0.0003.
Values sent between devices are 32-bit elements; how exact they have to be, the bound alone decides.
A program may use at most 128 MiB of HBM per device.

```python
import math
import jax
import jax.numpy as jnp
from jax import lax

N = 2048
LAYERS = 24


def shard_levels(own_key, shape, cuts, smallest, largest):
    factor_of = 1.0
    for position, parts in cuts:
        draws = jax.random.uniform(jax.random.fold_in(jax.random.fold_in(own_key, 6), position), (parts,), jnp.float32, smallest / len(cuts), largest / len(cuts))
        factor_of = factor_of * jnp.repeat(jnp.exp(draws), shape[position] // parts).reshape((-1,) + (1,) * (len(shape) - 1 - position))
    return factor_of


def scatter_about(own_key, shape, width, limit, cuts=(), held_as=jnp.bfloat16):
    values = width * jax.random.normal(own_key, shape, jnp.float32)
    if cuts:
        values = values * shard_levels(own_key, shape, cuts, -0.22, 0.18)
    return jnp.clip(values, -limit, limit).astype(held_as)


def setup_inputs(seed: int = 0) -> dict:
    seeds = jax.random.split(jax.random.key(seed), 5)
    return {
        "velocity": jnp.clip(1.5 + 4.5 * jax.random.uniform(seeds[0], (LAYERS, N, N), jnp.float32) ** shard_levels(seeds[0], (LAYERS, N, N), ((0, 8), (1, 32)), -0.2, 0.2), 1.5, 6.0),
        "dual_field": scatter_about(seeds[1], (3, LAYERS, N, N), 0.5, 3.0, ((1, 8), (2, 32)), jnp.float32),
        "kernel": jnp.clip(jnp.exp(math.log(5.0) - 2.3025851 * jax.random.uniform(seeds[2], (LAYERS, N, N), jnp.float32) ** shard_levels(seeds[2], (LAYERS, N, N), ((0, 8), (1, 32)), -0.2, 0.2)), 0.5, 5.0),
        "data_spec": scatter_about(seeds[3], (N, N), 2.0, 12.0, ((0, 32),), jnp.float32),
    }


gardner_coef = 1.741
dual_step = 0.25
primal_step = 0.25
tv_weight = 1.5
speed_floor = 1.5
speed_ceiling = 6.0

def hartley(values):
    length = values.shape[-1]
    first = jnp.fft.fft(values, axis=-1)
    values = first.real - first.imag
    second = jnp.fft.fft(values, axis=-2)
    return (second.real - second.imag) / length

def forward_diff(values, direction):
    length = values.shape[direction]
    following = lax.slice_in_dim(values, 1, length, axis=direction)
    closing = lax.slice_in_dim(values, length - 1, length, axis=direction)
    return jnp.concatenate([following, closing], axis=direction) - values

def last_mask(extent, direction):
    positions = lax.broadcasted_iota(jnp.int32, extent, direction)
    return positions < extent[direction] - 1

def backward_diff(values, direction):
    length = values.shape[direction]
    leading = jnp.zeros_like(lax.slice_in_dim(values, 0, 1, axis=direction))
    trimmed = lax.slice_in_dim(values, 0, length - 1, axis=direction)
    return values - jnp.concatenate([leading, trimmed], axis=direction)

def reference(velocity, dual_field, kernel, data_spec):
    density = gardner_coef * jnp.power(velocity, 0.25)
    spectra = jnp.swapaxes(hartley(density), 1, 2)
    summed = lax.optimization_barrier(jnp.sum(kernel * spectra, axis=0))
    misfit = (summed - data_spec).at[0, 0].set(0.0)
    adjoint = hartley(jnp.swapaxes(kernel * misfit[None], 1, 2))
    data_grad = 0.25 * density / velocity * adjoint
    components = []
    for component, direction in ((0, 1), (1, 2), (2, 0)):
        candidate = dual_field[component] + dual_step * forward_diff(velocity, direction)
        components.append(jnp.where(last_mask(velocity.shape, direction), candidate, 0.0))
    candidates = jnp.stack(components)
    magnitude = jnp.sqrt(lax.optimization_barrier(jnp.sum(candidates * candidates, axis=0)))
    dual_new = candidates / jnp.maximum(1.0, magnitude / tv_weight)
    divergence = backward_diff(dual_new[0], 1) + backward_diff(dual_new[1], 2) + backward_diff(dual_new[2], 0)
    update = velocity - primal_step * (data_grad - divergence)
    return (jnp.clip(update, speed_floor, speed_ceiling), dual_new)
```

```python
import functools
import math

import jax
import jax.numpy as jnp
import ml_dtypes
import numpy as np
from jax import lax
from jax.experimental import pallas as pl
from jax.experimental.pallas import tpu as pltpu
from jax.sharding import PartitionSpec as P

gardner_coef = 1.741
dual_step = 0.25
primal_step = 0.25
tv_weight = 1.5
speed_floor = 1.5
speed_ceiling = 6.0
density_shift = 2.326
chunks = 2
block = 256
MESH = pl.DeviceIdType.MESH
f32, bf16 = jnp.float32, jnp.bfloat16


def cas_parts(length):
    counter = np.arange(length, dtype=np.int64)
    angles = (counter[:, None] * counter[None, :] % length) * (2.0 * math.pi / length)
    matrix = ((np.cos(angles) + np.sin(angles)) / math.sqrt(length)).astype(np.float32)
    high = matrix.astype(ml_dtypes.bfloat16)
    low = (matrix - high.astype(np.float32)).astype(ml_dtypes.bfloat16)
    return high, low


def split(values):
    high = values.astype(bf16)
    return high, (values - high.astype(f32)).astype(bf16)


def dot(left, right):
    return jnp.dot(left, right, preferred_element_type=f32)


def step_kernel(
    planes, depths, size, layers,
    vel_in, dual_in, kern_in, data_in, ahi_in, alo_in,
    vel_out, dual_out,
    vel, dual, kern, data, ahi, alo, dt0h, dt0l, dt1h, dt1l,
    gsend, grecv, bsend, brecv, lhs, part, rsum, rrecv, zrecv, misfit, xt, acc, base,
    hsend, hrecv, psend, precv, layer_next, layer_prev,
    in_sem, a_sem, out_sem, gs_sem, gr_sem, bs_sem, br_sem, rs_sem, rr_sem, z_sem, ms_sem, mr_sem, h_sem,
):
    rows = size // planes
    span = rows // chunks
    half = span // 2
    slots = 2 * chunks
    group = min(8, planes)
    ny = depths // 2
    quarter = span // ny
    blocks = size // block
    per_block = block // rows
    me = lax.axis_index("plane")
    my_depth = lax.axis_index("depth")
    y, z = my_depth // 2, my_depth % 2
    home, seat = me // group, me % group

    def target(t):
        return ((home + t // group) % (planes // group)) * group + (seat + t % group) % group

    def y_peer(i):
        return ((y + i) % ny) * 2 + z

    after, before = (me + 1) % planes, (me + planes - 1) % planes
    above, below = (my_depth + 1) % depths, (my_depth + depths - 1) % depths
    sibling = y * 2 + (1 - z)
    diagonal = jnp.where(z == 0, below, above)

    loads = [
        pltpu.make_async_copy(src, dst, in_sem.at[i])
        for i, (src, dst) in enumerate(
            [(vel_in, vel.at[:, pl.ds(0, rows), :]), (dual_in, dual), (kern_in, kern), (data_in, data)]
        )
    ]
    loads[0].start()
    a_loads = [
        (
            pltpu.make_async_copy(ahi_in.at[:, s], ahi.at[:, s], a_sem.at[0, s]),
            pltpu.make_async_copy(alo_in.at[:, s], alo.at[:, s], a_sem.at[1, s]),
        )
        for s in range(slots)
    ]
    for pair in a_loads[:2]:
        for copy in pair:
            copy.start()
    loads[1].start()
    for pair in a_loads[2:]:
        for copy in pair:
            copy.start()
    loads[2].start()
    loads[3].start()

    barrier = pltpu.get_barrier_semaphore()

    def greet(t, _):
        pl.semaphore_signal(barrier, inc=1, device_id={"plane": target(t)}, device_id_type=MESH)
        return 0

    lax.fori_loop(1, planes, greet, 0)
    for i in range(1, ny):
        pl.semaphore_signal(barrier, inc=1, device_id={"depth": y_peer(i)}, device_id_type=MESH)
    pl.semaphore_signal(barrier, inc=1, device_id={"depth": sibling}, device_id_type=MESH)
    pl.semaphore_signal(barrier, inc=1, device_id={"depth": diagonal}, device_id_type=MESH)

    lane = lax.broadcasted_iota(jnp.int32, (half, 128), 1)
    left = lane < 64

    def swap(values):
        return pltpu.roll(values, 64, 1)

    loads[0].wait()

    def transpose_density(i, _):
        off = pl.multiple_of(i * 128, 128)
        where = pl.ds(off, 128)
        d = [gardner_coef * jnp.sqrt(jnp.sqrt(vel[l, 0:rows, where])) - density_shift for l in range(layers)]
        pair = jnp.concatenate([d[0], d[1]], axis=0).T
        third = jnp.concatenate([d[2], jnp.zeros_like(d[2])], axis=0).T
        pair_h, pair_l = split(pair)
        third_h, third_l = split(third)
        other_h, other_l = split(swap(third))
        dt0h[where, 0:128] = pair_h
        dt0l[where, 0:128] = pair_l
        dt1h[where, 0:128] = pair_h
        dt1l[where, 0:128] = pair_l
        dt0h[where, 128:256] = third_h
        dt0l[where, 128:256] = third_l
        dt1h[where, 128:256] = other_h
        dt1l[where, 128:256] = other_l
        return 0

    lax.fori_loop(0, size // 128, transpose_density, 0)
    for l in range(layers):
        hsend[l : l + 1, :] = vel[l, 0:1, :]
    for l in range(layers, 8):
        hsend[l : l + 1, :] = jnp.zeros((1, size), f32)

    pl.semaphore_wait(barrier, planes + ny)

    row_copy = pltpu.make_async_remote_copy(
        src_ref=hsend, dst_ref=hrecv, send_sem=h_sem.at[0], recv_sem=h_sem.at[1],
        device_id={"plane": before}, device_id_type=MESH)
    row_copy.start()
    layer_copy = pltpu.make_async_remote_copy(
        src_ref=vel_in.at[0], dst_ref=layer_next, send_sem=h_sem.at[2], recv_sem=h_sem.at[3],
        device_id={"depth": below}, device_id_type=MESH)
    layer_copy.start()

    def g_copy(k, t, who):
        to = target(t)
        return pltpu.make_async_remote_copy(
            src_ref=gsend.at[k, to], dst_ref=grecv.at[k, who], send_sem=gs_sem.at[k, to], recv_sem=gr_sem.at[k, who],
            device_id={"plane": to}, device_id_type=MESH)

    def b_copy(k, t, who):
        to = target(t)
        return pltpu.make_async_remote_copy(
            src_ref=bsend.at[k, to], dst_ref=brecv.at[k, who], send_sem=bs_sem.at[k, to], recv_sem=br_sem.at[k, who],
            device_id={"plane": to}, device_id_type=MESH)

    def columns(k, send):
        def one(g, _):
            first = pl.multiple_of(((home + g) % (planes // group)) * group, group)
            there = pl.ds(first, group)
            outs = []
            for h, (high, low) in enumerate([(dt0h, dt0l), (dt1h, dt1l)]):
                a_h = ahi[there, 2 * k + h].reshape(group * half, size)
                a_l = alo[there, 2 * k + h].reshape(group * half, size)
                both = dot(jnp.concatenate([a_h, a_l], axis=0), high[...])
                outs.append(both[: group * half] + both[group * half :] + dot(a_h, low[...]))
            gsend[k, there, :, 0:128] = outs[0][:, 0:128].reshape(group, half, 128)
            gsend[k, there, :, 128:256] = outs[1][:, 0:128].reshape(group, half, 128)
            gsend[k, there, :, 256:384] = (outs[0][:, 128:256] + outs[1][:, 128:256]).reshape(group, half, 128)
            if send:
                def start(t, _):
                    g_copy(k, t, me).start()
                    return 0

                lax.fori_loop(jnp.maximum(g * group, 1), (g + 1) * group, start, 0)
            return 0

        lax.fori_loop(0, planes // group, one, 0)
        grecv[k, me] = gsend[k, me]

    for pair in a_loads[:2]:
        for copy in pair:
            copy.wait()
    columns(0, True)
    for pair in a_loads[2:]:
        for copy in pair:
            copy.wait()
    columns(1, False)

    row8 = lax.broadcasted_iota(jnp.int32, (8, size), 0)
    col8 = lax.broadcasted_iota(jnp.int32, (8, size), 1)
    loads[1].wait()
    row_copy.wait()
    layer_copy.wait()
    for l in range(layers):
        vel[l, rows : rows + 1, :] = hrecv[l : l + 1, :]

    for l in range(layers):
        def dual_rows(i, _, l=l):
            off = pl.multiple_of(i * 8, 8)
            here = pl.ds(off, 8)
            v = vel[l, here, :]
            following = vel[l, pl.ds(pl.multiple_of(off + 8, 8), 8), :][0:1]
            next_row = jnp.where(row8 == 7, following, pltpu.roll(v, 7, 0))
            next_col = pltpu.roll(v, size - 1, 1)
            next_layer = vel[l + 1, here, :] if l + 1 < layers else layer_next[here, :]
            last_row = (me * rows + off + row8) == size - 1
            q0 = jnp.where(last_row, 0.0, dual[0, l, here, :] + dual_step * (next_row - v))
            q1 = jnp.where(col8 == size - 1, 0.0, dual[1, l, here, :] + dual_step * (next_col - v))
            q2 = dual[2, l, here, :] + dual_step * (next_layer - v)
            if l + 1 == layers:
                q2 = jnp.where(my_depth == depths - 1, 0.0, q2)
            scale = lax.rsqrt(jnp.maximum(1.0, (q0 * q0 + q1 * q1 + q2 * q2) * (1.0 / (tv_weight * tv_weight))))
            dual[0, l, here, :] = q0 * scale
            dual[1, l, here, :] = q1 * scale
            dual[2, l, here, :] = q2 * scale
            return 0

        lax.fori_loop(0, rows // 8, dual_rows, 0)
    for l in range(layers):
        psend[l : l + 1, :] = dual[0, l, rows - 1 : rows, :]
    for l in range(layers, 8):
        psend[l : l + 1, :] = jnp.zeros((1, size), f32)
    dual_store = pltpu.make_async_copy(dual, dual_out, out_sem.at[0])
    dual_store.start()
    prow_copy = pltpu.make_async_remote_copy(
        src_ref=psend, dst_ref=precv, send_sem=h_sem.at[4], recv_sem=h_sem.at[5],
        device_id={"plane": after}, device_id_type=MESH)
    prow_copy.start()
    player_copy = pltpu.make_async_remote_copy(
        src_ref=dual.at[2, layers - 1], dst_ref=layer_prev, send_sem=h_sem.at[6], recv_sem=h_sem.at[7],
        device_id={"depth": above}, device_id_type=MESH)
    player_copy.start()

    def g_next(t, _):
        g_copy(0, t, me).wait_send()
        g_copy(1, t, me).start()
        return 0

    lax.fori_loop(1, planes, g_next, 0)
    loads[2].wait()
    loads[3].wait()

    def rows_in(k):
        def arrived(t, _):
            g_copy(k, t, target(t)).wait_recv()
            return 0

        lax.fori_loop(1, planes, arrived, 0)

        def assemble(m, _):
            even, odd = grecv[k, 2 * m], grecv[k, 2 * m + 1]
            a, b, c = (even[:, 0:128], odd[:, 0:128]), (even[:, 128:256], odd[:, 128:256]), (even[:, 256:384], odd[:, 256:384])
            first = lambda p: jnp.where(left, p[0], swap(p[1]))
            second = lambda p: jnp.where(left, swap(p[0]), p[1])
            whole = jnp.concatenate([first(a), first(b), second(a), second(b), first(c), second(c)], axis=0)
            high, low = split(whole)
            there = pl.ds(pl.multiple_of(m * 128, 128), 128)
            lhs[0 : layers * span, there] = high
            lhs[layers * span : 2 * layers * span, there] = low
            return 0

        lax.fori_loop(0, planes // 2, assemble, 0)

    def times_matrix(n):
        there = pl.ds(pl.multiple_of(n * block, block), block)
        a_h = ahi[:, :, :, there].reshape(size, block)
        a_l = alo[:, :, :, there].reshape(size, block)
        count = layers * span
        both = dot(lhs[...], a_h)
        return there, both[:count] + both[count:] + dot(lhs[0:count, :], a_l)

    def weigh(k):
        def one(n, _):
            there, spectra = times_matrix(n)
            weights = kern[:, k * span : (k + 1) * span, there]
            part[k, :, there] = jnp.sum(weights * spectra.reshape(layers, span, block), axis=0)
            return 0

        lax.fori_loop(0, blocks, one, 0)

    def r_copy(k, i):
        to = (y + i) % ny
        return pltpu.make_async_remote_copy(
            src_ref=part.at[k, pl.ds(pl.multiple_of(to * quarter, quarter), quarter)], dst_ref=rrecv.at[k, i],
            send_sem=rs_sem.at[k, i], recv_sem=rr_sem.at[k, i],
            device_id={"depth": y_peer(i)}, device_id_type=MESH)

    def z_copy(k):
        return pltpu.make_async_remote_copy(
            src_ref=rsum.at[k], dst_ref=zrecv.at[k], send_sem=z_sem.at[0, k], recv_sem=z_sem.at[1, k],
            device_id={"depth": sibling}, device_id_type=MESH)

    mine = pl.ds(pl.multiple_of(y * quarter, quarter), quarter)

    def m_copy(k, i):
        return pltpu.make_async_remote_copy(
            src_ref=misfit.at[k, mine], dst_ref=misfit.at[k, mine],
            send_sem=ms_sem.at[k, i], recv_sem=mr_sem.at[k, i],
            device_id={"depth": y_peer(i)}, device_id_type=MESH)

    def m_arrival(k, i):
        theirs = pl.ds(pl.multiple_of(((y + ny - i) % ny) * quarter, quarter), quarter)
        return pltpu.make_async_remote_copy(
            src_ref=misfit.at[k, mine], dst_ref=misfit.at[k, theirs],
            send_sem=ms_sem.at[k, i], recv_sem=mr_sem.at[k, i],
            device_id={"depth": y_peer(i)}, device_id_type=MESH)

    def reduce_rows(k):
        total = part[k, mine, :]
        for i in range(1, ny):
            r_copy(k, i).wait_recv()
            total = total + rrecv[k, i]
        rsum[k] = total
        z_copy(k).start()

    def spread(k):
        z_copy(k).wait_recv()
        first = k * span + y * quarter
        summed = rsum[k] + zrecv[k]
        values = summed - data[pl.ds(pl.multiple_of(first, quarter), quarter), :]
        freq_col = me * rows + first + lax.broadcasted_iota(jnp.int32, (quarter, size), 0)
        freq_row = lax.broadcasted_iota(jnp.int32, (quarter, size), 1)
        misfit[k, mine, :] = jnp.where((freq_col == 0) & (freq_row == 0), 0.0, values)
        for i in range(1, ny):
            m_copy(k, i).start()

    def rows_out(k):
        for i in range(1, ny):
            m_arrival(k, i).wait_recv()
        count = layers * span

        def load(n, _):
            there = pl.ds(pl.multiple_of(n * block, block), block)
            weighted = kern[:, k * span : (k + 1) * span, there] * misfit[k, :, there][None]
            high, low = split(weighted.reshape(count, block))
            lhs[0:count, there] = high
            lhs[count : 2 * count, there] = low
            return 0

        lax.fori_loop(0, blocks, load, 0)
        left_all = lax.broadcasted_iota(jnp.int32, (layers, half, 128), 2) < 64

        def one(i, _):
            n = (home * (group // per_block) + i) % blocks
            _, values = times_matrix(n)
            for s in range(block // 128):
                slab = values[:, s * 128 : (s + 1) * 128].reshape(layers, 2, half, 128)
                top, low = slab[:, 0], slab[:, 1]
                even = jnp.where(left_all, top, pltpu.roll(low, 64, 2))
                odd = jnp.where(left_all, pltpu.roll(top, 64, 2), low)
                bsend[k, n * per_block + 2 * s] = even.reshape(layers * half, 128)
                bsend[k, n * per_block + 2 * s + 1] = odd.reshape(layers * half, 128)

            @pl.when(i % (group // per_block) == group // per_block - 1)
            def _():
                g = i // (group // per_block)

                def start(t, _):
                    b_copy(k, t, me).start()
                    return 0

                lax.fori_loop(jnp.maximum(g * group, 1), (g + 1) * group, start, 0)

            return 0

        lax.fori_loop(0, blocks, one, 0)
        brecv[k, me] = bsend[k, me]

    def columns_back(k, last):
        def arrived(t, _):
            b_copy(k, t, target(t)).wait_recv()
            return 0

        lax.fori_loop(1, planes, arrived, 0)
        high_rows = layers * rows
        many = 128 // half

        for l in range(layers):
            def turn(i, _, l=l):
                who = pl.ds(pl.multiple_of(i * many, many), many)
                tile = brecv[k, who, l * half : (l + 1) * half, :].reshape(128, 128).T
                high, low = split(tile)
                for h in range(2):
                    there = pl.ds(pl.multiple_of(h * planes * half + i * 128, 128), 128)
                    xt[l * rows : (l + 1) * rows, there] = high[h * 64 : (h + 1) * 64]
                    xt[high_rows + l * rows : high_rows + (l + 1) * rows, there] = low[h * 64 : (h + 1) * 64]
                return 0

            lax.fori_loop(0, planes // many, turn, 0)

        def one(n, _):
            there = pl.ds(pl.multiple_of(n * block, block), block)
            total = acc[:, there] if last else None
            for h in range(2):
                a_h = ahi[:, 2 * k + h, :, there].reshape(planes * half, block)
                a_l = alo[:, 2 * k + h, :, there].reshape(planes * half, block)
                part_x = xt[:, h * planes * half : (h + 1) * planes * half]
                both = dot(part_x, a_h)
                new = both[:high_rows] + both[high_rows:] + dot(part_x[:high_rows], a_l)
                total = new if total is None else total + new
            if last:
                adjoint = total.reshape(layers, rows, block)
                update = base[:, :, there] - vel[:, 0:rows, there] * adjoint
                base[:, :, there] = jnp.clip(update, speed_floor, speed_ceiling)
                pltpu.make_async_copy(base.at[:, :, there], vel_out.at[:, :, there], out_sem.at[1 + n]).start()
            else:
                acc[:, there] = total
            return 0

        lax.fori_loop(0, blocks, one, 0)

    rows_in(0)
    weigh(0)
    for i in range(1, ny):
        r_copy(0, i).start()

    prow_copy.wait()
    player_copy.wait()

    def diverge(half_range):
        for l in range(layers):
            def div_rows(i, _, l=l):
                off = pl.multiple_of(i * 8, 8)
                here = pl.ds(off, 8)
                previous = dual[0, l, pl.ds(pl.multiple_of(jnp.maximum(off - 8, 0), 8), 8), :][7:8]
                outer = jnp.where(me == 0, 0.0, precv[l : l + 1, :])
                leading = jnp.where(i == 0, outer, previous)
                p0, p1, p2 = dual[0, l, here, :], dual[1, l, here, :], dual[2, l, here, :]
                prev_row = jnp.where(row8 == 0, leading, pltpu.roll(p0, 1, 0))
                prev_col = jnp.where(col8 == 0, 0.0, pltpu.roll(p1, 1, 1))
                if l > 0:
                    prev_layer = dual[2, l - 1, here, :]
                else:
                    prev_layer = jnp.where(my_depth == 0, 0.0, layer_prev[here, :])
                divergence = (p0 - prev_row) + (p1 - prev_col) + (p2 - prev_layer)
                v = vel[l, here, :]
                base[l, here, :] = v + primal_step * divergence
                root = lax.rsqrt(v)
                vel[l, here, :] = (primal_step * 0.25 * gardner_coef) * (root * jnp.sqrt(root))
                return 0

            lax.fori_loop(0, rows // 8, div_rows, 0)

    reduce_rows(0)
    diverge(None)
    spread(0)
    rows_out(0)

    rows_in(1)
    weigh(1)
    for i in range(1, ny):
        r_copy(1, i).start()
    reduce_rows(1)
    spread(1)
    rows_out(1)
    columns_back(0, False)
    columns_back(1, True)

    def ended(t, _):
        g_copy(1, t, me).wait_send()
        b_copy(0, t, me).wait_send()
        b_copy(1, t, me).wait_send()
        return 0

    lax.fori_loop(1, planes, ended, 0)
    for k in range(chunks):
        z_copy(k).wait_send()
        for i in range(1, ny):
            r_copy(k, i).wait_send()
            m_copy(k, i).wait_send()
    dual_store.wait()

    def stored(n, _):
        there = pl.ds(pl.multiple_of(n * block, block), block)
        pltpu.make_async_copy(base.at[:, :, there], vel_out.at[:, :, there], out_sem.at[1 + n]).wait()
        return 0

    lax.fori_loop(0, blocks, stored, 0)


def body(velocity, dual_field, kernel, data_spec, high, low):
    planes = lax.axis_size("plane")
    depths = lax.axis_size("depth")
    layers, rows, size = velocity.shape
    span = rows // chunks
    half = span // 2
    ny = depths // 2
    quarter = span // ny
    hbm = pl.BlockSpec(memory_space=pltpu.HBM)
    vmem = pltpu.VMEM
    dma = pltpu.SemaphoreType.DMA
    scratch = [
        vmem((layers, rows + 8, size), f32),
        vmem((3, layers, rows, size), f32),
        vmem((layers, rows, size), f32),
        vmem((rows, size), f32),
        vmem((planes, 2 * chunks, half, size), bf16),
        vmem((planes, 2 * chunks, half, size), bf16),
        vmem((size, 256), bf16),
        vmem((size, 256), bf16),
        vmem((size, 256), bf16),
        vmem((size, 256), bf16),
        vmem((chunks, planes, half, 384), f32),
        vmem((chunks, planes, half, 384), f32),
        vmem((chunks, planes, layers * half, 128), f32),
        vmem((chunks, planes, layers * half, 128), f32),
        vmem((2 * layers * span, size), bf16),
        vmem((chunks, span, size), f32),
        vmem((chunks, quarter, size), f32),
        vmem((chunks, ny, quarter, size), f32),
        vmem((chunks, quarter, size), f32),
        vmem((chunks, span, size), f32),
        vmem((2 * layers * rows, 2 * planes * half), bf16),
        vmem((layers * rows, size), f32),
        vmem((layers, rows, size), f32),
        vmem((8, size), f32),
        vmem((8, size), f32),
        vmem((8, size), f32),
        vmem((8, size), f32),
        vmem((rows, size), f32),
        vmem((rows, size), f32),
        dma((4,)),
        dma((2, 2 * chunks)),
        dma((1 + size // block,)),
        dma((chunks, planes)),
        dma((chunks, planes)),
        dma((chunks, planes)),
        dma((chunks, planes)),
        dma((chunks, ny)),
        dma((chunks, ny)),
        dma((2, chunks)),
        dma((chunks, ny)),
        dma((chunks, ny)),
        dma((8,)),
    ]
    return pl.pallas_call(
        functools.partial(step_kernel, planes, depths, size, layers),
        out_shape=(
            jax.ShapeDtypeStruct(velocity.shape, f32),
            jax.ShapeDtypeStruct(dual_field.shape, f32),
        ),
        in_specs=[hbm] * 6,
        out_specs=(hbm, hbm),
        scratch_shapes=scratch,
        compiler_params=pltpu.CompilerParams(
            collective_id=0, has_side_effects=True, vmem_limit_bytes=60 * 1024 * 1024
        ),
        cost_estimate=pl.CostEstimate(
            flops=24 * layers * rows * size * size, bytes_accessed=60 * layers * rows * size, transcendentals=layers * rows * size
        ),
    )(velocity, dual_field, kernel, data_spec, high, low)


def solution(mesh):
    in_specs = (
        P("depth", "plane", None),
        P(None, "depth", "plane", None),
        P("depth", "plane", None),
        P("plane", None),
        P(),
        P(),
    )
    out_specs = (P("depth", "plane", None), P(None, "depth", "plane", None))
    mapped = jax.shard_map(body, mesh=mesh, in_specs=in_specs, out_specs=out_specs, check_vma=False)

    def run(velocity, dual_field, kernel, data_spec):
        size, planes = velocity.shape[-1], mesh.shape["plane"]
        shape = (planes, 2 * chunks, size // planes // (2 * chunks), size)
        high, low = (part.reshape(shape) for part in cas_parts(size))
        return mapped(velocity, dual_field, kernel, data_spec, jnp.asarray(high), jnp.asarray(low))

    return run
```

```python
import functools
import math

import jax
import jax.numpy as jnp
import ml_dtypes
import numpy as np
from jax import lax
from jax.experimental import pallas as pl
from jax.experimental.pallas import tpu as pltpu
from jax.sharding import PartitionSpec as P

gardner_coef = 1.741
dual_step = 0.25
primal_step = 0.25
tv_weight = 1.5
speed_floor = 1.5
speed_ceiling = 6.0
density_shift = 2.326
chunks = 2
block = 256
MESH = pl.DeviceIdType.MESH
f32, bf16 = jnp.float32, jnp.bfloat16


def cas_parts(length):
    counter = np.arange(length, dtype=np.int64)
    angles = (counter[:, None] * counter[None, :] % length) * (2.0 * math.pi / length)
    matrix = ((np.cos(angles) + np.sin(angles)) / math.sqrt(length)).astype(np.float32)
    high = matrix.astype(ml_dtypes.bfloat16)
    low = (matrix - high.astype(np.float32)).astype(ml_dtypes.bfloat16)
    return high, low


def split(values):
    high = values.astype(bf16)
    return high, (values - high.astype(f32)).astype(bf16)


def dot(left, right):
    return jnp.dot(left, right, preferred_element_type=f32)


def step_kernel(
    planes, depths, size, layers,
    vel_in, dual_in, kern_in, data_in, ahi_in, alo_in,
    base, dual,
    vel, kern, data, ahi, alo, dt0h, dt0l, dt1h, dt1l,
    gsend, grecv, bsend, brecv, lhs, part, rsum, rrecv, zrecv, misfit, xt, acc, spec,
    hsend, hrecv, psend, precv, layer_next, layer_prev,
    in_sem, a_sem, gs_sem, gr_sem, bs_sem, br_sem, rs_sem, rr_sem, z_sem, ms_sem, mr_sem, h_sem,
):
    rows = size // planes
    span = rows // chunks
    half = span // 2
    slots = 2 * chunks
    group = min(8, planes)
    ny = depths // 2
    quarter = span // ny
    blocks = size // block
    per_block = block // rows
    me = lax.axis_index("plane")
    my_depth = lax.axis_index("depth")
    y, z = my_depth // 2, my_depth % 2
    home, seat = me // group, me % group

    def target(t):
        return ((home + t // group) % (planes // group)) * group + (seat + t % group) % group

    def y_peer(i):
        return ((y + i) % ny) * 2 + z

    after, before = (me + 1) % planes, (me + planes - 1) % planes
    above, below = (my_depth + 1) % depths, (my_depth + depths - 1) % depths
    sibling = y * 2 + (1 - z)
    diagonal = jnp.where(z == 0, below, above)

    loads = [
        pltpu.make_async_copy(src, dst, in_sem.at[i])
        for i, (src, dst) in enumerate(
            [(vel_in, vel.at[:, pl.ds(0, rows), :]), (dual_in, dual), (kern_in, kern), (data_in, data)]
        )
    ]
    loads[0].start()
    a_loads = [
        (
            pltpu.make_async_copy(ahi_in.at[:, s], ahi.at[:, s], a_sem.at[0, s]),
            pltpu.make_async_copy(alo_in.at[:, s], alo.at[:, s], a_sem.at[1, s]),
        )
        for s in range(slots)
    ]
    for pair in a_loads[:2]:
        for copy in pair:
            copy.start()
    loads[1].start()
    for pair in a_loads[2:]:
        for copy in pair:
            copy.start()
    loads[2].start()
    loads[3].start()

    barrier = pltpu.get_barrier_semaphore()

    def greet(t, _):
        pl.semaphore_signal(barrier, inc=1, device_id={"plane": target(t)}, device_id_type=MESH)
        return 0

    lax.fori_loop(1, planes, greet, 0)
    for i in range(1, ny):
        pl.semaphore_signal(barrier, inc=1, device_id={"depth": y_peer(i)}, device_id_type=MESH)
    pl.semaphore_signal(barrier, inc=1, device_id={"depth": sibling}, device_id_type=MESH)
    pl.semaphore_signal(barrier, inc=1, device_id={"depth": diagonal}, device_id_type=MESH)

    lane = lax.broadcasted_iota(jnp.int32, (half, 128), 1)
    left = lane < 64

    def swap(values):
        return pltpu.roll(values, 64, 1)

    loads[0].wait()

    def transpose_density(i, _):
        off = pl.multiple_of(i * 128, 128)
        where = pl.ds(off, 128)
        d = [gardner_coef * jnp.sqrt(jnp.sqrt(vel[l, 0:rows, where])) - density_shift for l in range(layers)]
        pair = jnp.concatenate([d[0], d[1]], axis=0).T
        third = jnp.concatenate([d[2], jnp.zeros_like(d[2])], axis=0).T
        pair_h, pair_l = split(pair)
        third_h, third_l = split(third)
        other_h, other_l = split(swap(third))
        dt0h[where, 0:128] = pair_h
        dt0l[where, 0:128] = pair_l
        dt1h[where, 0:128] = pair_h
        dt1l[where, 0:128] = pair_l
        dt0h[where, 128:256] = third_h
        dt0l[where, 128:256] = third_l
        dt1h[where, 128:256] = other_h
        dt1l[where, 128:256] = other_l
        return 0

    lax.fori_loop(0, size // 128, transpose_density, 0)
    for l in range(layers):
        hsend[l : l + 1, :] = vel[l, 0:1, :]
    for l in range(layers, 8):
        hsend[l : l + 1, :] = jnp.zeros((1, size), f32)

    pl.semaphore_wait(barrier, planes + ny)

    row_copy = pltpu.make_async_remote_copy(
        src_ref=hsend, dst_ref=hrecv, send_sem=h_sem.at[0], recv_sem=h_sem.at[1],
        device_id={"plane": before}, device_id_type=MESH)
    row_copy.start()
    layer_copy = pltpu.make_async_remote_copy(
        src_ref=vel_in.at[0], dst_ref=layer_next, send_sem=h_sem.at[2], recv_sem=h_sem.at[3],
        device_id={"depth": below}, device_id_type=MESH)

    def g_copy(k, t, who):
        to = target(t)
        return pltpu.make_async_remote_copy(
            src_ref=gsend.at[k, to], dst_ref=grecv.at[k, who], send_sem=gs_sem.at[k, to], recv_sem=gr_sem.at[k, who],
            device_id={"plane": to}, device_id_type=MESH)

    def b_copy(k, t, who):
        to = target(t)
        return pltpu.make_async_remote_copy(
            src_ref=bsend.at[k, to], dst_ref=brecv.at[k, who], send_sem=bs_sem.at[k, to], recv_sem=br_sem.at[k, who],
            device_id={"plane": to}, device_id_type=MESH)

    def columns(k, send):
        def one(g, _):
            first = pl.multiple_of(((home + g) % (planes // group)) * group, group)
            there = pl.ds(first, group)
            outs = []
            for h, (high, low) in enumerate([(dt0h, dt0l), (dt1h, dt1l)]):
                a_h = ahi[there, 2 * k + h].reshape(group * half, size)
                a_l = alo[there, 2 * k + h].reshape(group * half, size)
                both = dot(jnp.concatenate([a_h, a_l], axis=0), high[...])
                outs.append(both[: group * half] + both[group * half :] + dot(a_h, low[...]))
            gsend[k, there, :, 0:128] = outs[0][:, 0:128].reshape(group, half, 128)
            gsend[k, there, :, 128:256] = outs[1][:, 0:128].reshape(group, half, 128)
            gsend[k, there, :, 256:384] = (outs[0][:, 128:256] + outs[1][:, 128:256]).reshape(group, half, 128)
            if send:
                def start(t, _):
                    g_copy(k, t, me).start()
                    return 0

                lax.fori_loop(jnp.maximum(g * group, 1), (g + 1) * group, start, 0)
            return 0

        lax.fori_loop(0, planes // group, one, 0)
        grecv[k, me] = gsend[k, me]

    for pair in a_loads[:2]:
        for copy in pair:
            copy.wait()
    columns(0, True)
    for pair in a_loads[2:]:
        for copy in pair:
            copy.wait()
    columns(1, False)

    loads[2].wait()
    loads[3].wait()

    groups = planes // group
    wide = group * rows

    def g_arrival(k, t, who):
        return pltpu.make_async_remote_copy(
            src_ref=gsend.at[k, who], dst_ref=grecv.at[k, who], send_sem=gs_sem.at[k, who], recv_sem=gr_sem.at[k, who],
            device_id={"plane": who}, device_id_type=MESH)

    def b_arrival(k, t, who):
        return pltpu.make_async_remote_copy(
            src_ref=bsend.at[k, who], dst_ref=brecv.at[k, who], send_sem=bs_sem.at[k, who], recv_sem=br_sem.at[k, who],
            device_id={"plane": who}, device_id_type=MESH)

    def source_group(g):
        return (home + groups - g) % groups

    def sources(g, arrival, k):
        owner = source_group(g)

        def arrived(i, _):
            arrival(k, 0, owner * group + (seat + i) % group).wait_recv()
            return 0

        lax.fori_loop(jnp.where(g == 0, 1, 0), group, arrived, 0)

    def g_start(k, g):
        def start(t, _):
            g_copy(k, t, me).start()
            return 0

        lax.fori_loop(max(g * group, 1), (g + 1) * group, start, 0)

    def b_start(k, first, last):
        def start(t, _):
            b_copy(k, t, me).start()
            return 0

        lax.fori_loop(first, last, start, 0)

    count = layers * span

    def group_planes(g):
        return pl.ds(pl.multiple_of(source_group(g) * group, group), group)

    def rows_in(k, some, then=()):
        for g in some:
            sources(g, g_arrival, k)
            if g < len(then) and then[g] is not None:
                g_start(1, then[g])

            def assemble(i, _, g=g):
                m = source_group(g) * (group // 2) + i
                even, odd = grecv[k, 2 * m], grecv[k, 2 * m + 1]
                a, b, c = (even[:, 0:128], odd[:, 0:128]), (even[:, 128:256], odd[:, 128:256]), (even[:, 256:384], odd[:, 256:384])
                first = lambda p: jnp.where(left, p[0], swap(p[1]))
                second = lambda p: jnp.where(left, swap(p[0]), p[1])
                whole = jnp.concatenate([first(a), first(b), second(a), second(b), first(c), second(c)], axis=0)
                high, low = split(whole)
                there = pl.ds(pl.multiple_of(g * wide + i * 128, 128), 128)
                lhs[0:count, there] = high
                lhs[count : 2 * count, there] = low
                return 0

            lax.fori_loop(0, group // 2, assemble, 0)
        last = some[-1] + 1 == groups

        def one(n, _):
            there = pl.ds(pl.multiple_of(n * block, block), block)
            spectra = spec[:, there] if some[0] > 0 else None
            for g in some:
                a_h = ahi[group_planes(g), :, :, there].reshape(wide, block)
                a_l = alo[group_planes(g), :, :, there].reshape(wide, block)
                both = dot(lhs[:, g * wide : (g + 1) * wide], a_h)
                new = both[:count] + both[count:] + dot(lhs[0:count, g * wide : (g + 1) * wide], a_l)
                spectra = new if spectra is None else spectra + new
            if last:
                weights = kern[:, k * span : (k + 1) * span, there]
                part[k, :, there] = jnp.sum(weights * spectra.reshape(layers, span, block), axis=0)
            else:
                spec[:, there] = spectra
            return 0

        lax.fori_loop(0, blocks, one, 0)
        if last:
            for i in range(1, ny):
                r_copy(k, i).start()

    def times_matrix(n):
        there = pl.ds(pl.multiple_of(n * block, block), block)
        a_h = ahi[:, :, :, there].reshape(size, block)
        a_l = alo[:, :, :, there].reshape(size, block)
        both = dot(lhs[...], a_h)
        return both[:count] + both[count:] + dot(lhs[0:count, :], a_l)

    def r_copy(k, i):
        to = (y + i) % ny
        return pltpu.make_async_remote_copy(
            src_ref=part.at[k, pl.ds(pl.multiple_of(to * quarter, quarter), quarter)], dst_ref=rrecv.at[k, i],
            send_sem=rs_sem.at[k, i], recv_sem=rr_sem.at[k, i],
            device_id={"depth": y_peer(i)}, device_id_type=MESH)

    def z_copy(k):
        return pltpu.make_async_remote_copy(
            src_ref=rsum.at[k], dst_ref=zrecv.at[k], send_sem=z_sem.at[0, k], recv_sem=z_sem.at[1, k],
            device_id={"depth": sibling}, device_id_type=MESH)

    mine = pl.ds(pl.multiple_of(y * quarter, quarter), quarter)

    def m_copy(k, i):
        return pltpu.make_async_remote_copy(
            src_ref=misfit.at[k, mine], dst_ref=misfit.at[k, mine],
            send_sem=ms_sem.at[k, i], recv_sem=mr_sem.at[k, i],
            device_id={"depth": y_peer(i)}, device_id_type=MESH)

    def m_arrival(k, i):
        theirs = pl.ds(pl.multiple_of(((y + ny - i) % ny) * quarter, quarter), quarter)
        return pltpu.make_async_remote_copy(
            src_ref=misfit.at[k, mine], dst_ref=misfit.at[k, theirs],
            send_sem=ms_sem.at[k, i], recv_sem=mr_sem.at[k, i],
            device_id={"depth": y_peer(i)}, device_id_type=MESH)

    def reduce_rows(k):
        total = part[k, mine, :]
        for i in range(1, ny):
            r_copy(k, i).wait_recv()
            total = total + rrecv[k, i]
        rsum[k] = total
        z_copy(k).start()

    def spread(k):
        z_copy(k).wait_recv()
        first = k * span + y * quarter
        summed = rsum[k] + zrecv[k]
        values = summed - data[pl.ds(pl.multiple_of(first, quarter), quarter), :]
        freq_col = me * rows + first + lax.broadcasted_iota(jnp.int32, (quarter, size), 0)
        freq_row = lax.broadcasted_iota(jnp.int32, (quarter, size), 1)
        misfit[k, mine, :] = jnp.where((freq_col == 0) & (freq_row == 0), 0.0, values)
        for i in range(1, ny):
            m_copy(k, i).start()

    def weigh_misfit(k):
        for i in range(1, ny):
            m_arrival(k, i).wait_recv()

        def load(n, _):
            there = pl.ds(pl.multiple_of(n * block, block), block)
            weighted = kern[:, k * span : (k + 1) * span, there] * misfit[k, :, there][None]
            high, low = split(weighted.reshape(count, block))
            lhs[0:count, there] = high
            lhs[count : 2 * count, there] = low
            return 0

        lax.fori_loop(0, blocks, load, 0)

    left_all = lax.broadcasted_iota(jnp.int32, (layers, half, 128), 2) < 64

    def rows_out(k, begin, end):
        def one(i, _):
            n = (home * (group // per_block) + i) % blocks
            values = times_matrix(n)
            for s in range(block // 128):
                slab = values[:, s * 128 : (s + 1) * 128].reshape(layers, 2, half, 128)
                top, low = slab[:, 0], slab[:, 1]
                even = jnp.where(left_all, top, pltpu.roll(low, 64, 2))
                odd = jnp.where(left_all, pltpu.roll(top, 64, 2), low)
                bsend[k, n * per_block + 2 * s] = even.reshape(layers * half, 128)
                bsend[k, n * per_block + 2 * s + 1] = odd.reshape(layers * half, 128)

            @pl.when(i % (group // per_block) == group // per_block - 1)
            def _():
                g = i // (group // per_block)
                b_start(k, jnp.maximum(g * group, 1), (g + 1) * group)

            return 0

        lax.fori_loop(begin, end, one, 0)
        if begin == 0:
            brecv[k, me] = bsend[k, me]

    high_rows = layers * rows
    tile_rows = group * half

    def columns_back(k, some):
        for g in some:
            sources(g, b_arrival, k)
            for l in range(layers):
                tile = brecv[k, group_planes(g), l * half : (l + 1) * half, :].reshape(tile_rows, 128).T
                high, low = split(tile)
                for h in range(2):
                    there = pl.ds((2 * g + h) * tile_rows, tile_rows)
                    xt[l * rows : (l + 1) * rows, there] = high[h * 64 : (h + 1) * 64]
                    xt[high_rows + l * rows : high_rows + (l + 1) * rows, there] = low[h * 64 : (h + 1) * 64]
        first, final = k == 0 and some[0] == 0, k + 1 == chunks and some[-1] + 1 == groups

        def one(n, _):
            there = pl.ds(pl.multiple_of(n * block, block), block)
            total = None if first else acc[:, there]
            for g in some:
                a_h = jnp.concatenate([ahi[group_planes(g), 2 * k + h, :, there].reshape(tile_rows, block) for h in range(2)], axis=0)
                a_l = jnp.concatenate([alo[group_planes(g), 2 * k + h, :, there].reshape(tile_rows, block) for h in range(2)], axis=0)
                where = pl.ds(2 * g * tile_rows, 2 * tile_rows)
                both = dot(xt[:, where], a_h)
                new = both[:high_rows] + both[high_rows:] + dot(xt[0:high_rows, where], a_l)
                total = new if total is None else total + new
            if final:
                adjoint = total.reshape(layers, rows, block)
                update = base[:, :, there] - vel[:, 0:rows, there] * adjoint
                base[:, :, there] = jnp.clip(update, speed_floor, speed_ceiling)
            else:
                acc[:, there] = total
            return 0

        lax.fori_loop(0, blocks, one, 0)

    prow_copy = pltpu.make_async_remote_copy(
        src_ref=psend, dst_ref=precv, send_sem=h_sem.at[4], recv_sem=h_sem.at[5],
        device_id={"plane": after}, device_id_type=MESH)
    player_copy = pltpu.make_async_remote_copy(
        src_ref=dual.at[2, layers - 1], dst_ref=layer_prev, send_sem=h_sem.at[6], recv_sem=h_sem.at[7],
        device_id={"depth": above}, device_id_type=MESH)

    row8 = lax.broadcasted_iota(jnp.int32, (8, size), 0)
    col8 = lax.broadcasted_iota(jnp.int32, (8, size), 1)

    def update_dual():
        loads[1].wait()
        row_copy.wait()
        layer_copy.wait()
        for l in range(layers):
            vel[l, rows : rows + 1, :] = hrecv[l : l + 1, :]

        for l in range(layers):
            def dual_rows(i, _, l=l):
                off = pl.multiple_of(i * 8, 8)
                here = pl.ds(off, 8)
                v = vel[l, here, :]
                following = vel[l, pl.ds(pl.multiple_of(off + 8, 8), 8), :][0:1]
                next_row = jnp.where(row8 == 7, following, pltpu.roll(v, 7, 0))
                next_col = pltpu.roll(v, size - 1, 1)
                next_layer = vel[l + 1, here, :] if l + 1 < layers else layer_next[here, :]
                last_row = (me * rows + off + row8) == size - 1
                q0 = jnp.where(last_row, 0.0, dual[0, l, here, :] + dual_step * (next_row - v))
                q1 = jnp.where(col8 == size - 1, 0.0, dual[1, l, here, :] + dual_step * (next_col - v))
                q2 = dual[2, l, here, :] + dual_step * (next_layer - v)
                if l + 1 == layers:
                    q2 = jnp.where(my_depth == depths - 1, 0.0, q2)
                scale = lax.rsqrt(jnp.maximum(1.0, (q0 * q0 + q1 * q1 + q2 * q2) * (1.0 / (tv_weight * tv_weight))))
                dual[0, l, here, :] = q0 * scale
                dual[1, l, here, :] = q1 * scale
                dual[2, l, here, :] = q2 * scale
                return 0

            lax.fori_loop(0, rows // 8, dual_rows, 0)
        for l in range(layers):
            psend[l : l + 1, :] = dual[0, l, rows - 1 : rows, :]
        for l in range(layers, 8):
            psend[l : l + 1, :] = jnp.zeros((1, size), f32)
    def diverge():
        prow_copy.wait()
        player_copy.wait()
        for l in range(layers):
            def div_rows(i, _, l=l):
                off = pl.multiple_of(i * 8, 8)
                here = pl.ds(off, 8)
                previous = dual[0, l, pl.ds(pl.multiple_of(jnp.maximum(off - 8, 0), 8), 8), :][7:8]
                outer = jnp.where(me == 0, 0.0, precv[l : l + 1, :])
                leading = jnp.where(i == 0, outer, previous)
                p0, p1, p2 = dual[0, l, here, :], dual[1, l, here, :], dual[2, l, here, :]
                prev_row = jnp.where(row8 == 0, leading, pltpu.roll(p0, 1, 0))
                prev_col = jnp.where(col8 == 0, 0.0, pltpu.roll(p1, 1, 1))
                if l > 0:
                    prev_layer = dual[2, l - 1, here, :]
                else:
                    prev_layer = jnp.where(my_depth == 0, 0.0, layer_prev[here, :])
                divergence = (p0 - prev_row) + (p1 - prev_col) + (p2 - prev_layer)
                v = vel[l, here, :]
                base[l, here, :] = v + primal_step * divergence
                root = lax.rsqrt(v)
                vel[l, here, :] = (primal_step * 0.25 * gardner_coef) * (root * jnp.sqrt(root))
                return 0

            lax.fori_loop(0, rows // 8, div_rows, 0)

    early, late = tuple(range(groups - 1)), (groups - 1,)
    rows_in(0, early, (0, 1))
    rows_in(0, late, (None,) * (groups - 1) + (2,))
    reduce_rows(0)
    g_start(1, 3)
    layer_copy.start()
    rows_in(1, early)
    spread(0)
    rows_in(1, late)
    weigh_misfit(0)
    rows_out(0, 0, blocks // 2)
    reduce_rows(1)
    rows_out(0, blocks // 2, blocks)
    update_dual()
    prow_copy.start()
    player_copy.start()
    spread(1)
    weigh_misfit(1)
    rows_out(1, 0, blocks)
    columns_back(0, early + late)
    diverge()
    columns_back(1, early)
    columns_back(1, late)

    def ended(t, _):
        g_copy(0, t, me).wait_send()
        g_copy(1, t, me).wait_send()
        b_copy(0, t, me).wait_send()
        b_copy(1, t, me).wait_send()
        return 0

    lax.fori_loop(1, planes, ended, 0)
    for k in range(chunks):
        z_copy(k).wait_send()
        for i in range(1, ny):
            r_copy(k, i).wait_send()
            m_copy(k, i).wait_send()


def store_kernel(vel, dual, vel_out, dual_out, sem):
    copies = [pltpu.make_async_copy(dual.at[c], dual_out.at[c], sem.at[c]) for c in range(3)]
    copies.append(pltpu.make_async_copy(vel, vel_out, sem.at[3]))
    for copy in copies:
        copy.start()
    for copy in copies:
        copy.wait()


def body(velocity, dual_field, kernel, data_spec, high, low):
    planes = lax.axis_size("plane")
    depths = lax.axis_size("depth")
    layers, rows, size = velocity.shape
    span = rows // chunks
    half = span // 2
    ny = depths // 2
    quarter = span // ny
    hbm = pl.BlockSpec(memory_space=pltpu.HBM)
    vmem = pltpu.VMEM
    dma = pltpu.SemaphoreType.DMA
    scratch = [
        vmem((layers, rows + 8, size), f32),
        vmem((layers, rows, size), f32),
        vmem((rows, size), f32),
        vmem((planes, 2 * chunks, half, size), bf16),
        vmem((planes, 2 * chunks, half, size), bf16),
        vmem((size, 256), bf16),
        vmem((size, 256), bf16),
        vmem((size, 256), bf16),
        vmem((size, 256), bf16),
        vmem((chunks, planes, half, 384), f32),
        vmem((chunks, planes, half, 384), f32),
        vmem((chunks, planes, layers * half, 128), f32),
        vmem((chunks, planes, layers * half, 128), f32),
        vmem((2 * layers * span, size), bf16),
        vmem((chunks, span, size), f32),
        vmem((chunks, quarter, size), f32),
        vmem((chunks, ny, quarter, size), f32),
        vmem((chunks, quarter, size), f32),
        vmem((chunks, span, size), f32),
        vmem((2 * layers * rows, 2 * planes * half), bf16),
        vmem((layers * rows, size), f32),
        vmem((layers * span, size), f32),
        vmem((8, size), f32),
        vmem((8, size), f32),
        vmem((8, size), f32),
        vmem((8, size), f32),
        vmem((rows, size), f32),
        vmem((rows, size), f32),
        dma((4,)),
        dma((2, 2 * chunks)),
        dma((chunks, planes)),
        dma((chunks, planes)),
        dma((chunks, planes)),
        dma((chunks, planes)),
        dma((chunks, ny)),
        dma((chunks, ny)),
        dma((2, chunks)),
        dma((chunks, ny)),
        dma((chunks, ny)),
        dma((8,)),
    ]
    on_chip = pl.BlockSpec(memory_space=vmem)
    updated = pl.pallas_call(
        functools.partial(step_kernel, planes, depths, size, layers),
        out_shape=(vmem(velocity.shape, f32), vmem(dual_field.shape, f32)),
        in_specs=[hbm] * 6,
        out_specs=(on_chip, on_chip),
        scratch_shapes=scratch,
        compiler_params=pltpu.CompilerParams(
            collective_id=0, has_side_effects=True, vmem_limit_bytes=48 * 1024 * 1024
        ),
        cost_estimate=pl.CostEstimate(
            flops=24 * layers * rows * size * size, bytes_accessed=60 * layers * rows * size, transcendentals=layers * rows * size
        ),
    )(velocity, dual_field, kernel, data_spec, high, low)
    return pl.pallas_call(
        store_kernel,
        out_shape=(
            jax.ShapeDtypeStruct(velocity.shape, f32),
            jax.ShapeDtypeStruct(dual_field.shape, f32),
        ),
        in_specs=[on_chip, on_chip],
        out_specs=(hbm, hbm),
        scratch_shapes=[dma((4,))],
        compiler_params=pltpu.CompilerParams(has_side_effects=True, vmem_limit_bytes=8 * 1024 * 1024),
    )(*updated)


def solution(mesh):
    in_specs = (
        P("depth", "plane", None),
        P(None, "depth", "plane", None),
        P("depth", "plane", None),
        P("plane", None),
        P(),
        P(),
    )
    out_specs = (P("depth", "plane", None), P(None, "depth", "plane", None))
    mapped = jax.shard_map(body, mesh=mesh, in_specs=in_specs, out_specs=out_specs, check_vma=False)

    def run(velocity, dual_field, kernel, data_spec):
        size, planes = velocity.shape[-1], mesh.shape["plane"]
        shape = (planes, 2 * chunks, size // planes // (2 * chunks), size)
        high, low = (part.reshape(shape) for part in cas_parts(size))
        return mapped(velocity, dual_field, kernel, data_spec, jnp.asarray(high), jnp.asarray(low))

    return run
```

```python
import functools
import math

import jax
import jax.numpy as jnp
import ml_dtypes
import numpy as np
from jax import lax
from jax.experimental import pallas as pl
from jax.experimental.pallas import tpu as pltpu
from jax.sharding import PartitionSpec as P

gardner_coef = 1.741
dual_step = 0.25
primal_step = 0.25
tv_weight = 1.5
speed_floor = 1.5
speed_ceiling = 6.0
density_shift = 2.326
chunks = 2
block = 256
MESH = pl.DeviceIdType.MESH
f32, bf16 = jnp.float32, jnp.bfloat16


def cas_parts(length):
    counter = np.arange(length, dtype=np.int64)
    angles = (counter[:, None] * counter[None, :] % length) * (2.0 * math.pi / length)
    matrix = ((np.cos(angles) + np.sin(angles)) / math.sqrt(length)).astype(np.float32)
    high = matrix.astype(ml_dtypes.bfloat16)
    low = (matrix - high.astype(np.float32)).astype(ml_dtypes.bfloat16)
    return high, low


def split(values):
    high = values.astype(bf16)
    return high, (values - high.astype(f32)).astype(bf16)


def dot(left, right):
    return jnp.dot(left, right, preferred_element_type=f32)


def step_kernel(
    planes, depths, size, layers,
    vel_in, dual_in, kern_in, data_in, ahi_in, alo_in,
    base, dual,
    vel, kern, data, ahi, alo, dt0h, dt0l, dt1h, dt1l,
    gsend, grecv, bsend, brecv, lhs, part, rsum, rrecv, zrecv, misfit, xt, acc, spec,
    hsend, hrecv, psend, precv, layer_next, layer_prev,
    in_sem, a_sem, gs_sem, gr_sem, bs_sem, br_sem, rs_sem, rr_sem, z_sem, ms_sem, mr_sem, h_sem,
):
    rows = size // planes
    span = rows // chunks
    half = span // 2
    slots = 2 * chunks
    group = min(8, planes)
    ny = depths // 2
    quarter = span // ny
    blocks = size // block
    per_block = block // rows
    me = lax.axis_index("plane")
    my_depth = lax.axis_index("depth")
    y, z = my_depth // 2, my_depth % 2
    home, seat = me // group, me % group

    def target(t):
        return ((home + t // group) % (planes // group)) * group + (seat + t % group) % group

    def y_peer(i):
        return ((y + i) % ny) * 2 + z

    after, before = (me + 1) % planes, (me + planes - 1) % planes
    above, below = (my_depth + 1) % depths, (my_depth + depths - 1) % depths
    sibling = y * 2 + (1 - z)
    diagonal = jnp.where(z == 0, below, above)

    loads = [
        pltpu.make_async_copy(src, dst, in_sem.at[i])
        for i, (src, dst) in enumerate(
            [(vel_in, vel.at[:, pl.ds(0, rows), :]), (dual_in, dual), (kern_in, kern), (data_in, data)]
        )
    ]
    loads[0].start()
    a_loads = [
        (
            pltpu.make_async_copy(ahi_in.at[:, s], ahi.at[:, s], a_sem.at[0, s]),
            pltpu.make_async_copy(alo_in.at[:, s], alo.at[:, s], a_sem.at[1, s]),
        )
        for s in range(slots)
    ]
    for pair in a_loads[:2]:
        for copy in pair:
            copy.start()
    loads[1].start()
    for pair in a_loads[2:]:
        for copy in pair:
            copy.start()
    loads[2].start()
    loads[3].start()

    barrier = pltpu.get_barrier_semaphore()

    def greet(t, _):
        pl.semaphore_signal(barrier, inc=1, device_id={"plane": target(t)}, device_id_type=MESH)
        return 0

    lax.fori_loop(1, planes, greet, 0)
    for i in range(1, ny):
        pl.semaphore_signal(barrier, inc=1, device_id={"depth": y_peer(i)}, device_id_type=MESH)
    pl.semaphore_signal(barrier, inc=1, device_id={"depth": sibling}, device_id_type=MESH)
    pl.semaphore_signal(barrier, inc=1, device_id={"depth": diagonal}, device_id_type=MESH)

    lane = lax.broadcasted_iota(jnp.int32, (half, 128), 1)
    left = lane < 64

    def swap(values):
        return pltpu.roll(values, 64, 1)

    loads[0].wait()

    def transpose_density(i, _):
        off = pl.multiple_of(i * 128, 128)
        where = pl.ds(off, 128)
        d = [gardner_coef * jnp.sqrt(jnp.sqrt(vel[l, 0:rows, where])) - density_shift for l in range(layers)]
        pair = jnp.concatenate([d[0], d[1]], axis=0).T
        third = jnp.concatenate([d[2], jnp.zeros_like(d[2])], axis=0).T
        pair_h, pair_l = split(pair)
        third_h, third_l = split(third)
        other_h, other_l = split(swap(third))
        dt0h[where, 0:128] = pair_h
        dt0l[where, 0:128] = pair_l
        dt1h[where, 0:128] = pair_h
        dt1l[where, 0:128] = pair_l
        dt0h[where, 128:256] = third_h
        dt0l[where, 128:256] = third_l
        dt1h[where, 128:256] = other_h
        dt1l[where, 128:256] = other_l
        return 0

    lax.fori_loop(0, size // 128, transpose_density, 0)
    for l in range(layers):
        hsend[l : l + 1, :] = vel[l, 0:1, :]
    for l in range(layers, 8):
        hsend[l : l + 1, :] = jnp.zeros((1, size), f32)

    row_copy = pltpu.make_async_remote_copy(
        src_ref=hsend, dst_ref=hrecv, send_sem=h_sem.at[0], recv_sem=h_sem.at[1],
        device_id={"plane": before}, device_id_type=MESH)
    layer_copy = pltpu.make_async_remote_copy(
        src_ref=vel_in.at[0], dst_ref=layer_next, send_sem=h_sem.at[2], recv_sem=h_sem.at[3],
        device_id={"depth": below}, device_id_type=MESH)

    def g_copy(k, t, who):
        to = target(t)
        return pltpu.make_async_remote_copy(
            src_ref=gsend.at[k, to], dst_ref=grecv.at[k, who], send_sem=gs_sem.at[k, to], recv_sem=gr_sem.at[k, who],
            device_id={"plane": to}, device_id_type=MESH)

    def b_copy(k, t, who):
        to = target(t)
        return pltpu.make_async_remote_copy(
            src_ref=bsend.at[k, to], dst_ref=brecv.at[k, who], send_sem=bs_sem.at[k, to], recv_sem=br_sem.at[k, who],
            device_id={"plane": to}, device_id_type=MESH)

    def g_start(k, g):
        def start(t, _):
            g_copy(k, t, me).start()
            return 0

        lax.fori_loop(max(g * group, 1), (g + 1) * group, start, 0)

    def columns(k, send, begin, end):
        def one(g, _):
            first = pl.multiple_of(((home + g) % (planes // group)) * group, group)
            there = pl.ds(first, group)
            outs = []
            for h, (high, low) in enumerate([(dt0h, dt0l), (dt1h, dt1l)]):
                a_h = ahi[there, 2 * k + h].reshape(group * half, size)
                a_l = alo[there, 2 * k + h].reshape(group * half, size)
                both = dot(jnp.concatenate([a_h, a_l], axis=0), high[...])
                outs.append(both[: group * half] + both[group * half :] + dot(a_h, low[...]))
            gsend[k, there, :, 0:128] = outs[0][:, 0:128].reshape(group, half, 128)
            gsend[k, there, :, 128:256] = outs[1][:, 0:128].reshape(group, half, 128)
            gsend[k, there, :, 256:384] = (outs[0][:, 128:256] + outs[1][:, 128:256]).reshape(group, half, 128)
            if send:
                def start(t, _):
                    g_copy(k, t, me).start()
                    return 0

                lax.fori_loop(jnp.maximum(g * group, 1), (g + 1) * group, start, 0)
            return 0

        lax.fori_loop(begin, end, one, 0)
        if begin == 0:
            grecv[k, me] = gsend[k, me]

    for pair in a_loads[:2]:
        for copy in pair:
            copy.wait()
    columns(0, False, 0, 1)
    pl.semaphore_wait(barrier, planes + ny)
    g_start(0, 0)
    columns(0, True, 1, planes // group)
    row_copy.start()
    for pair in a_loads[2:]:
        for copy in pair:
            copy.wait()
    columns(1, False, 0, planes // group)

    loads[2].wait()
    loads[3].wait()

    groups = planes // group
    wide = group * rows

    def g_arrival(k, t, who):
        return pltpu.make_async_remote_copy(
            src_ref=gsend.at[k, who], dst_ref=grecv.at[k, who], send_sem=gs_sem.at[k, who], recv_sem=gr_sem.at[k, who],
            device_id={"plane": who}, device_id_type=MESH)

    def b_arrival(k, t, who):
        return pltpu.make_async_remote_copy(
            src_ref=bsend.at[k, who], dst_ref=brecv.at[k, who], send_sem=bs_sem.at[k, who], recv_sem=br_sem.at[k, who],
            device_id={"plane": who}, device_id_type=MESH)

    def source_group(g):
        return (home + groups - g) % groups

    def sources(g, arrival, k):
        owner = source_group(g)

        def arrived(i, _):
            arrival(k, 0, owner * group + (seat + i) % group).wait_recv()
            return 0

        lax.fori_loop(jnp.where(g == 0, 1, 0), group, arrived, 0)

    def b_start(k, first, last):
        def start(t, _):
            b_copy(k, t, me).start()
            return 0

        lax.fori_loop(first, last, start, 0)

    count = layers * span

    def group_planes(g):
        return pl.ds(pl.multiple_of(source_group(g) * group, group), group)

    def rows_in(k, some, then=()):
        for g in some:
            sources(g, g_arrival, k)
            if g < len(then) and then[g] is not None:
                g_start(1, then[g])

            def assemble(i, _, g=g):
                m = source_group(g) * (group // 2) + i
                even, odd = grecv[k, 2 * m], grecv[k, 2 * m + 1]
                a, b, c = (even[:, 0:128], odd[:, 0:128]), (even[:, 128:256], odd[:, 128:256]), (even[:, 256:384], odd[:, 256:384])
                first = lambda p: jnp.where(left, p[0], swap(p[1]))
                second = lambda p: jnp.where(left, swap(p[0]), p[1])
                whole = jnp.concatenate([first(a), first(b), second(a), second(b), first(c), second(c)], axis=0)
                high, low = split(whole)
                there = pl.ds(pl.multiple_of(g * wide + i * 128, 128), 128)
                lhs[0:count, there] = high
                lhs[count : 2 * count, there] = low
                return 0

            lax.fori_loop(0, group // 2, assemble, 0)
        last = some[-1] + 1 == groups

        def one(n, _):
            there = pl.ds(pl.multiple_of(n * block, block), block)
            spectra = spec[:, there] if some[0] > 0 else None
            for g in some:
                a_h = ahi[group_planes(g), :, :, there].reshape(wide, block)
                a_l = alo[group_planes(g), :, :, there].reshape(wide, block)
                both = dot(lhs[:, g * wide : (g + 1) * wide], a_h)
                new = both[:count] + both[count:] + dot(lhs[0:count, g * wide : (g + 1) * wide], a_l)
                spectra = new if spectra is None else spectra + new
            if last:
                weights = kern[:, k * span : (k + 1) * span, there]
                part[k, :, there] = jnp.sum(weights * spectra.reshape(layers, span, block), axis=0)
            else:
                spec[:, there] = spectra
            return 0

        lax.fori_loop(0, blocks, one, 0)
        if last:
            for i in range(1, ny):
                r_copy(k, i).start()

    def times_matrix(n):
        there = pl.ds(pl.multiple_of(n * block, block), block)
        a_h = ahi[:, :, :, there].reshape(size, block)
        a_l = alo[:, :, :, there].reshape(size, block)
        both = dot(lhs[...], a_h)
        return both[:count] + both[count:] + dot(lhs[0:count, :], a_l)

    def r_copy(k, i):
        to = (y + i) % ny
        return pltpu.make_async_remote_copy(
            src_ref=part.at[k, pl.ds(pl.multiple_of(to * quarter, quarter), quarter)], dst_ref=rrecv.at[k, i],
            send_sem=rs_sem.at[k, i], recv_sem=rr_sem.at[k, i],
            device_id={"depth": y_peer(i)}, device_id_type=MESH)

    def z_copy(k):
        return pltpu.make_async_remote_copy(
            src_ref=rsum.at[k], dst_ref=zrecv.at[k], send_sem=z_sem.at[0, k], recv_sem=z_sem.at[1, k],
            device_id={"depth": sibling}, device_id_type=MESH)

    mine = pl.ds(pl.multiple_of(y * quarter, quarter), quarter)

    def m_copy(k, i):
        return pltpu.make_async_remote_copy(
            src_ref=misfit.at[k, mine], dst_ref=misfit.at[k, mine],
            send_sem=ms_sem.at[k, i], recv_sem=mr_sem.at[k, i],
            device_id={"depth": y_peer(i)}, device_id_type=MESH)

    def m_arrival(k, i):
        theirs = pl.ds(pl.multiple_of(((y + ny - i) % ny) * quarter, quarter), quarter)
        return pltpu.make_async_remote_copy(
            src_ref=misfit.at[k, mine], dst_ref=misfit.at[k, theirs],
            send_sem=ms_sem.at[k, i], recv_sem=mr_sem.at[k, i],
            device_id={"depth": y_peer(i)}, device_id_type=MESH)

    def reduce_rows(k):
        total = part[k, mine, :]
        for i in range(1, ny):
            r_copy(k, i).wait_recv()
            total = total + rrecv[k, i]
        rsum[k] = total
        z_copy(k).start()

    def spread(k):
        z_copy(k).wait_recv()
        first = k * span + y * quarter
        summed = rsum[k] + zrecv[k]
        values = summed - data[pl.ds(pl.multiple_of(first, quarter), quarter), :]
        freq_col = me * rows + first + lax.broadcasted_iota(jnp.int32, (quarter, size), 0)
        freq_row = lax.broadcasted_iota(jnp.int32, (quarter, size), 1)
        misfit[k, mine, :] = jnp.where((freq_col == 0) & (freq_row == 0), 0.0, values)
        for i in range(1, ny):
            m_copy(k, i).start()

    def weigh_misfit(k):
        for i in range(1, ny):
            m_arrival(k, i).wait_recv()

        def load(n, _):
            there = pl.ds(pl.multiple_of(n * block, block), block)
            weighted = kern[:, k * span : (k + 1) * span, there] * misfit[k, :, there][None]
            high, low = split(weighted.reshape(count, block))
            lhs[0:count, there] = high
            lhs[count : 2 * count, there] = low
            return 0

        lax.fori_loop(0, blocks, load, 0)

    left_all = lax.broadcasted_iota(jnp.int32, (layers, half, 128), 2) < 64

    def rows_out(k, begin, end):
        def one(i, _):
            n = (home * (group // per_block) + i) % blocks
            values = times_matrix(n)
            for s in range(block // 128):
                slab = values[:, s * 128 : (s + 1) * 128].reshape(layers, 2, half, 128)
                top, low = slab[:, 0], slab[:, 1]
                even = jnp.where(left_all, top, pltpu.roll(low, 64, 2))
                odd = jnp.where(left_all, pltpu.roll(top, 64, 2), low)
                bsend[k, n * per_block + 2 * s] = even.reshape(layers * half, 128)
                bsend[k, n * per_block + 2 * s + 1] = odd.reshape(layers * half, 128)

            @pl.when(i % (group // per_block) == group // per_block - 1)
            def _():
                g = i // (group // per_block)
                b_start(k, jnp.maximum(g * group, 1), (g + 1) * group)

            return 0

        lax.fori_loop(begin, end, one, 0)
        if begin == 0:
            brecv[k, me] = bsend[k, me]

    high_rows = layers * rows
    tile_rows = group * half

    def columns_back(k, some):
        for g in some:
            sources(g, b_arrival, k)
            for l in range(layers):
                tile = brecv[k, group_planes(g), l * half : (l + 1) * half, :].reshape(tile_rows, 128).T
                high, low = split(tile)
                for h in range(2):
                    there = pl.ds((2 * g + h) * tile_rows, tile_rows)
                    xt[l * rows : (l + 1) * rows, there] = high[h * 64 : (h + 1) * 64]
                    xt[high_rows + l * rows : high_rows + (l + 1) * rows, there] = low[h * 64 : (h + 1) * 64]
        first = k == 0 and some[0] == 0

        def one(n, _):
            there = pl.ds(pl.multiple_of(n * block, block), block)
            total = None if first else acc[:, there]
            for g in some:
                a_h = jnp.concatenate([ahi[group_planes(g), 2 * k + h, :, there].reshape(tile_rows, block) for h in range(2)], axis=0)
                a_l = jnp.concatenate([alo[group_planes(g), 2 * k + h, :, there].reshape(tile_rows, block) for h in range(2)], axis=0)
                where = pl.ds(2 * g * tile_rows, 2 * tile_rows)
                both = dot(xt[:, where], a_h)
                new = both[:high_rows] + both[high_rows:] + dot(xt[0:high_rows, where], a_l)
                total = new if total is None else total + new
            acc[:, there] = total
            return 0

        lax.fori_loop(0, blocks, one, 0)

    prow_copy = pltpu.make_async_remote_copy(
        src_ref=psend, dst_ref=precv, send_sem=h_sem.at[4], recv_sem=h_sem.at[5],
        device_id={"plane": after}, device_id_type=MESH)
    part_rows = rows // 2
    player_copies = [
        pltpu.make_async_remote_copy(
            src_ref=dual.at[2, layers - 1, pl.ds(h * part_rows, part_rows)],
            dst_ref=layer_prev.at[pl.ds(h * part_rows, part_rows)],
            send_sem=h_sem.at[6 + 2 * h], recv_sem=h_sem.at[7 + 2 * h],
            device_id={"depth": above}, device_id_type=MESH)
        for h in range(2)
    ]

    row8 = lax.broadcasted_iota(jnp.int32, (8, size), 0)
    col8 = lax.broadcasted_iota(jnp.int32, (8, size), 1)

    def update_dual():
        loads[1].wait()
        row_copy.wait()
        layer_copy.wait()
        for l in range(layers):
            vel[l, rows : rows + 1, :] = hrecv[l : l + 1, :]

        for l in range(layers):
            def dual_rows(i, _, l=l):
                off = pl.multiple_of(i * 8, 8)
                here = pl.ds(off, 8)
                v = vel[l, here, :]
                following = vel[l, pl.ds(pl.multiple_of(off + 8, 8), 8), :][0:1]
                next_row = jnp.where(row8 == 7, following, pltpu.roll(v, 7, 0))
                next_col = pltpu.roll(v, size - 1, 1)
                next_layer = vel[l + 1, here, :] if l + 1 < layers else layer_next[here, :]
                last_row = (me * rows + off + row8) == size - 1
                q0 = jnp.where(last_row, 0.0, dual[0, l, here, :] + dual_step * (next_row - v))
                q1 = jnp.where(col8 == size - 1, 0.0, dual[1, l, here, :] + dual_step * (next_col - v))
                q2 = dual[2, l, here, :] + dual_step * (next_layer - v)
                if l + 1 == layers:
                    q2 = jnp.where(my_depth == depths - 1, 0.0, q2)
                scale = lax.rsqrt(jnp.maximum(1.0, (q0 * q0 + q1 * q1 + q2 * q2) * (1.0 / (tv_weight * tv_weight))))
                dual[0, l, here, :] = q0 * scale
                dual[1, l, here, :] = q1 * scale
                dual[2, l, here, :] = q2 * scale
                return 0

            lax.fori_loop(0, rows // 8, dual_rows, 0)
        for l in range(layers):
            psend[l : l + 1, :] = dual[0, l, rows - 1 : rows, :]
        for l in range(layers, 8):
            psend[l : l + 1, :] = jnp.zeros((1, size), f32)
    def diverge(some, begin, end):
        for l in some:
            def div_rows(i, _, l=l):
                off = pl.multiple_of(i * 8, 8)
                here = pl.ds(off, 8)
                previous = dual[0, l, pl.ds(pl.multiple_of(jnp.maximum(off - 8, 0), 8), 8), :][7:8]
                outer = jnp.where(me == 0, 0.0, precv[l : l + 1, :])
                leading = jnp.where(i == 0, outer, previous)
                p0, p1, p2 = dual[0, l, here, :], dual[1, l, here, :], dual[2, l, here, :]
                prev_row = jnp.where(row8 == 0, leading, pltpu.roll(p0, 1, 0))
                prev_col = jnp.where(col8 == 0, 0.0, pltpu.roll(p1, 1, 1))
                if l > 0:
                    prev_layer = dual[2, l - 1, here, :]
                else:
                    prev_layer = jnp.where(my_depth == 0, 0.0, layer_prev[here, :])
                divergence = (p0 - prev_row) + (p1 - prev_col) + (p2 - prev_layer)
                v = vel[l, here, :]
                base[l, here, :] = v + primal_step * divergence
                root = lax.rsqrt(v)
                vel[l, here, :] = (primal_step * 0.25 * gardner_coef) * (root * jnp.sqrt(root))
                return 0

            lax.fori_loop(begin, end, div_rows, 0)

    early, late = tuple(range(groups - 1)), (groups - 1,)
    def update_velocity(some, begin, end):
        for l in some:
            def new_rows(i, _, l=l):
                here = pl.ds(pl.multiple_of(i * 8, 8), 8)
                there = pl.ds(pl.multiple_of(l * rows + i * 8, 8), 8)
                update = base[l, here, :] - vel[l, here, :] * acc[there, :]
                base[l, here, :] = jnp.clip(update, speed_floor, speed_ceiling)
                return 0

            lax.fori_loop(begin, end, new_rows, 0)

    rows_in(0, early, tuple(range(groups - 1)))
    rows_in(0, late, (None,) * (groups - 1) + (groups - 1,))
    reduce_rows(0)
    layer_copy.start()
    rows_in(1, early)
    spread(0)
    rows_in(1, late)
    weigh_misfit(0)
    rows_out(0, 0, blocks // 2)
    reduce_rows(1)
    rows_out(0, blocks // 2, blocks)
    update_dual()
    prow_copy.start()
    spread(1)
    weigh_misfit(1)
    rows_out(1, 0, blocks)
    player_copies[0].start()
    player_copies[1].start()
    columns_back(0, early + late)
    prow_copy.wait()
    diverge(range(1, layers), 0, rows // 8)
    columns_back(1, early)
    columns_back(1, late)
    update_velocity(range(1, layers), 0, rows // 8)
    player_copies[0].wait()
    diverge((0,), 0, rows // 16)
    update_velocity((0,), 0, rows // 16)
    player_copies[1].wait()
    diverge((0,), rows // 16, rows // 8)
    update_velocity((0,), rows // 16, rows // 8)

    def ended(t, _):
        g_copy(0, t, me).wait_send()
        g_copy(1, t, me).wait_send()
        b_copy(0, t, me).wait_send()
        b_copy(1, t, me).wait_send()
        return 0

    lax.fori_loop(1, planes, ended, 0)
    for k in range(chunks):
        z_copy(k).wait_send()
        for i in range(1, ny):
            r_copy(k, i).wait_send()
            m_copy(k, i).wait_send()


def store_kernel(vel, dual, vel_out, dual_out, sem):
    layers = vel.shape[0]
    copies = [
        pltpu.make_async_copy(dual.at[c, l], dual_out.at[c, l], sem.at[c, l]) for c in range(3) for l in range(layers)
    ]
    copies += [pltpu.make_async_copy(vel.at[l], vel_out.at[l], sem.at[3, l]) for l in range(layers)]
    for copy in copies:
        copy.start()
    for copy in copies:
        copy.wait()


def body(velocity, dual_field, kernel, data_spec, high, low):
    planes = lax.axis_size("plane")
    depths = lax.axis_size("depth")
    layers, rows, size = velocity.shape
    span = rows // chunks
    half = span // 2
    ny = depths // 2
    quarter = span // ny
    hbm = pl.BlockSpec(memory_space=pltpu.HBM)
    vmem = pltpu.VMEM
    dma = pltpu.SemaphoreType.DMA
    scratch = [
        vmem((layers, rows + 8, size), f32),
        vmem((layers, rows, size), f32),
        vmem((rows, size), f32),
        vmem((planes, 2 * chunks, half, size), bf16),
        vmem((planes, 2 * chunks, half, size), bf16),
        vmem((size, 256), bf16),
        vmem((size, 256), bf16),
        vmem((size, 256), bf16),
        vmem((size, 256), bf16),
        vmem((chunks, planes, half, 384), f32),
        vmem((chunks, planes, half, 384), f32),
        vmem((chunks, planes, layers * half, 128), f32),
        vmem((chunks, planes, layers * half, 128), f32),
        vmem((2 * layers * span, size), bf16),
        vmem((chunks, span, size), f32),
        vmem((chunks, quarter, size), f32),
        vmem((chunks, ny, quarter, size), f32),
        vmem((chunks, quarter, size), f32),
        vmem((chunks, span, size), f32),
        vmem((2 * layers * rows, 2 * planes * half), bf16),
        vmem((layers * rows, size), f32),
        vmem((layers * span, size), f32),
        vmem((8, size), f32),
        vmem((8, size), f32),
        vmem((8, size), f32),
        vmem((8, size), f32),
        vmem((rows, size), f32),
        vmem((rows, size), f32),
        dma((4,)),
        dma((2, 2 * chunks)),
        dma((chunks, planes)),
        dma((chunks, planes)),
        dma((chunks, planes)),
        dma((chunks, planes)),
        dma((chunks, ny)),
        dma((chunks, ny)),
        dma((2, chunks)),
        dma((chunks, ny)),
        dma((chunks, ny)),
        dma((10,)),
    ]
    on_chip = pl.BlockSpec(memory_space=vmem)
    updated = pl.pallas_call(
        functools.partial(step_kernel, planes, depths, size, layers),
        out_shape=(vmem(velocity.shape, f32), vmem(dual_field.shape, f32)),
        in_specs=[hbm] * 6,
        out_specs=(on_chip, on_chip),
        scratch_shapes=scratch,
        compiler_params=pltpu.CompilerParams(
            collective_id=0, has_side_effects=True, vmem_limit_bytes=48 * 1024 * 1024
        ),
        cost_estimate=pl.CostEstimate(
            flops=24 * layers * rows * size * size, bytes_accessed=60 * layers * rows * size, transcendentals=layers * rows * size
        ),
    )(velocity, dual_field, kernel, data_spec, high, low)
    return pl.pallas_call(
        store_kernel,
        out_shape=(
            jax.ShapeDtypeStruct(velocity.shape, f32),
            jax.ShapeDtypeStruct(dual_field.shape, f32),
        ),
        in_specs=[on_chip, on_chip],
        out_specs=(hbm, hbm),
        scratch_shapes=[dma((4, layers))],
        compiler_params=pltpu.CompilerParams(has_side_effects=True, vmem_limit_bytes=8 * 1024 * 1024),
    )(*updated)


def solution(mesh):
    in_specs = (
        P("depth", "plane", None),
        P(None, "depth", "plane", None),
        P("depth", "plane", None),
        P("plane", None),
        P(),
        P(),
    )
    out_specs = (P("depth", "plane", None), P(None, "depth", "plane", None))
    mapped = jax.shard_map(body, mesh=mesh, in_specs=in_specs, out_specs=out_specs, check_vma=False)

    def run(velocity, dual_field, kernel, data_spec):
        size, planes = velocity.shape[-1], mesh.shape["plane"]
        shape = (planes, 2 * chunks, size // planes // (2 * chunks), size)
        high, low = (part.reshape(shape) for part in cas_parts(size))
        return mapped(velocity, dual_field, kernel, data_spec, jnp.asarray(high), jnp.asarray(low))

    return run
```

```python
import functools
import math

import jax
import jax.numpy as jnp
import ml_dtypes
import numpy as np
from jax import lax
from jax.experimental import pallas as pl
from jax.experimental.pallas import tpu as pltpu
from jax.sharding import PartitionSpec as P

gardner_coef = 1.741
dual_step = 0.25
primal_step = 0.25
tv_weight = 1.5
speed_floor = 1.5
speed_ceiling = 6.0
density_shift = 2.326
chunks = 2
block = 256
MESH = pl.DeviceIdType.MESH
f32, bf16 = jnp.float32, jnp.bfloat16


def cas_parts(length):
    counter = np.arange(length, dtype=np.int64)
    angles = (counter[:, None] * counter[None, :] % length) * (2.0 * math.pi / length)
    matrix = ((np.cos(angles) + np.sin(angles)) / math.sqrt(length)).astype(np.float32)
    high = matrix.astype(ml_dtypes.bfloat16)
    low = (matrix - high.astype(np.float32)).astype(ml_dtypes.bfloat16)
    return high, low


def split(values):
    high = values.astype(bf16)
    return high, (values - high.astype(f32)).astype(bf16)


def dot(left, right):
    return jnp.dot(left, right, preferred_element_type=f32)


def step_kernel(
    planes, depths, size, layers,
    vel_in, dual_in, kern_in, data_in, ahi_in, alo_in,
    base, dual,
    vel, kern, data, ahi, alo, dt0h, dt0l, dt1h, dt1l,
    gsend, grecv, bsend, brecv, lhs, part, rsum, rrecv, zrecv, misfit, xt, acc, spec,
    hsend, hrecv, psend, precv, layer_next, layer_prev,
    in_sem, a_sem, gs_sem, gr_sem, bs_sem, br_sem, rs_sem, rr_sem, z_sem, ms_sem, mr_sem, h_sem,
):
    rows = size // planes
    span = rows // chunks
    half = span // 2
    slots = 2 * chunks
    group = min(8, planes)
    ny = depths // 2
    quarter = span // ny
    blocks = size // block
    per_block = block // rows
    me = lax.axis_index("plane")
    my_depth = lax.axis_index("depth")
    y, z = my_depth // 2, my_depth % 2
    home, seat = me // group, me % group

    def target(t):
        return ((home + t // group) % (planes // group)) * group + (seat + t % group) % group

    def y_peer(i):
        return ((y + i) % ny) * 2 + z

    after, before = (me + 1) % planes, (me + planes - 1) % planes
    above, below = (my_depth + 1) % depths, (my_depth + depths - 1) % depths
    sibling = y * 2 + (1 - z)
    diagonal = jnp.where(z == 0, below, above)

    loads = [
        pltpu.make_async_copy(src, dst, in_sem.at[i])
        for i, (src, dst) in enumerate(
            [(vel_in, vel.at[:, pl.ds(0, rows), :]), (dual_in, dual), (kern_in, kern), (data_in, data)]
        )
    ]
    loads[0].start()
    a_loads = [
        (
            pltpu.make_async_copy(ahi_in.at[:, s], ahi.at[:, s], a_sem.at[0, s]),
            pltpu.make_async_copy(alo_in.at[:, s], alo.at[:, s], a_sem.at[1, s]),
        )
        for s in range(slots)
    ]
    for pair in a_loads[:2]:
        for copy in pair:
            copy.start()
    loads[1].start()
    for pair in a_loads[2:]:
        for copy in pair:
            copy.start()
    loads[2].start()
    loads[3].start()

    barrier = pltpu.get_barrier_semaphore()

    def greet(t, _):
        pl.semaphore_signal(barrier, inc=1, device_id={"plane": target(t)}, device_id_type=MESH)
        return 0

    lax.fori_loop(1, planes, greet, 0)
    for i in range(1, ny):
        pl.semaphore_signal(barrier, inc=1, device_id={"depth": y_peer(i)}, device_id_type=MESH)
    pl.semaphore_signal(barrier, inc=1, device_id={"depth": sibling}, device_id_type=MESH)
    pl.semaphore_signal(barrier, inc=1, device_id={"depth": diagonal}, device_id_type=MESH)

    lane = lax.broadcasted_iota(jnp.int32, (half, 128), 1)
    left = lane < 64

    def swap(values):
        return pltpu.roll(values, 64, 1)

    loads[0].wait()

    def transpose_density(i, _):
        off = pl.multiple_of(i * 128, 128)
        where = pl.ds(off, 128)
        d = [gardner_coef * jnp.sqrt(jnp.sqrt(vel[l, 0:rows, where])) - density_shift for l in range(layers)]
        pair = jnp.concatenate([d[0], d[1]], axis=0).T
        third = jnp.concatenate([d[2], jnp.zeros_like(d[2])], axis=0).T
        pair_h, pair_l = split(pair)
        third_h, third_l = split(third)
        other_h, other_l = split(swap(third))
        dt0h[where, 0:128] = pair_h
        dt0l[where, 0:128] = pair_l
        dt1h[where, 0:128] = pair_h
        dt1l[where, 0:128] = pair_l
        dt0h[where, 128:256] = third_h
        dt0l[where, 128:256] = third_l
        dt1h[where, 128:256] = other_h
        dt1l[where, 128:256] = other_l
        return 0

    lax.fori_loop(0, size // 128, transpose_density, 0)
    for l in range(layers):
        hsend[l : l + 1, :] = vel[l, 0:1, :]
    for l in range(layers, 8):
        hsend[l : l + 1, :] = jnp.zeros((1, size), f32)

    row_copy = pltpu.make_async_remote_copy(
        src_ref=hsend, dst_ref=hrecv, send_sem=h_sem.at[0], recv_sem=h_sem.at[1],
        device_id={"plane": before}, device_id_type=MESH)
    layer_copy = pltpu.make_async_remote_copy(
        src_ref=vel_in.at[0], dst_ref=layer_next, send_sem=h_sem.at[2], recv_sem=h_sem.at[3],
        device_id={"depth": below}, device_id_type=MESH)

    def g_copy(k, t, who):
        to = target(t)
        return pltpu.make_async_remote_copy(
            src_ref=gsend.at[k, to], dst_ref=grecv.at[k, who], send_sem=gs_sem.at[k, to], recv_sem=gr_sem.at[k, who],
            device_id={"plane": to}, device_id_type=MESH)

    def b_copy(k, t, who):
        to = target(t)
        return pltpu.make_async_remote_copy(
            src_ref=bsend.at[k, to], dst_ref=brecv.at[k, who], send_sem=bs_sem.at[k, to], recv_sem=br_sem.at[k, who],
            device_id={"plane": to}, device_id_type=MESH)

    def g_start(k, g):
        def start(t, _):
            g_copy(k, t, me).start()
            return 0

        lax.fori_loop(max(g * group, 1), (g + 1) * group, start, 0)

    def columns(k, send, begin, end):
        def one(g, _):
            first = pl.multiple_of(((home + g) % (planes // group)) * group, group)
            there = pl.ds(first, group)
            outs = []
            for h, (high, low) in enumerate([(dt0h, dt0l), (dt1h, dt1l)]):
                a_h = ahi[there, 2 * k + h].reshape(group * half, size)
                a_l = alo[there, 2 * k + h].reshape(group * half, size)
                both = dot(jnp.concatenate([a_h, a_l], axis=0), high[...])
                outs.append(both[: group * half] + both[group * half :] + dot(a_h, low[...]))
            gsend[k, there, :, 0:128] = outs[0][:, 0:128].reshape(group, half, 128)
            gsend[k, there, :, 128:256] = outs[1][:, 0:128].reshape(group, half, 128)
            gsend[k, there, :, 256:384] = (outs[0][:, 128:256] + outs[1][:, 128:256]).reshape(group, half, 128)
            if send:
                def start(t, _):
                    g_copy(k, t, me).start()
                    return 0

                lax.fori_loop(jnp.maximum(g * group, 1), (g + 1) * group, start, 0)
            return 0

        lax.fori_loop(begin, end, one, 0)
        if begin == 0:
            grecv[k, me] = gsend[k, me]

    for pair in a_loads[:2]:
        for copy in pair:
            copy.wait()
    columns(0, False, 0, 1)
    pl.semaphore_wait(barrier, planes + ny)
    g_start(0, 0)
    columns(0, True, 1, planes // group)
    row_copy.start()
    for pair in a_loads[2:]:
        for copy in pair:
            copy.wait()
    columns(1, False, 0, planes // group)

    loads[2].wait()
    loads[3].wait()

    groups = planes // group
    wide = group * rows

    def g_arrival(k, t, who):
        return pltpu.make_async_remote_copy(
            src_ref=gsend.at[k, who], dst_ref=grecv.at[k, who], send_sem=gs_sem.at[k, who], recv_sem=gr_sem.at[k, who],
            device_id={"plane": who}, device_id_type=MESH)

    def b_arrival(k, t, who):
        return pltpu.make_async_remote_copy(
            src_ref=bsend.at[k, who], dst_ref=brecv.at[k, who], send_sem=bs_sem.at[k, who], recv_sem=br_sem.at[k, who],
            device_id={"plane": who}, device_id_type=MESH)

    def source_group(g):
        return (home + groups - g) % groups

    def sources(g, arrival, k):
        owner = source_group(g)

        def arrived(i, _):
            arrival(k, 0, owner * group + (seat + i) % group).wait_recv()
            return 0

        lax.fori_loop(jnp.where(g == 0, 1, 0), group, arrived, 0)

    def b_start(k, first, last):
        def start(t, _):
            b_copy(k, t, me).start()
            return 0

        lax.fori_loop(first, last, start, 0)

    count = layers * span

    def group_planes(g):
        return pl.ds(pl.multiple_of(source_group(g) * group, group), group)

    def rows_in(k, some, then=()):
        for g in some:
            sources(g, g_arrival, k)
            if g < len(then) and then[g] is not None:
                g_start(1, then[g])

            def assemble(i, _, g=g):
                m = source_group(g) * (group // 2) + i
                even, odd = grecv[k, 2 * m], grecv[k, 2 * m + 1]
                a, b, c = (even[:, 0:128], odd[:, 0:128]), (even[:, 128:256], odd[:, 128:256]), (even[:, 256:384], odd[:, 256:384])
                first = lambda p: jnp.where(left, p[0], swap(p[1]))
                second = lambda p: jnp.where(left, swap(p[0]), p[1])
                whole = jnp.concatenate([first(a), first(b), second(a), second(b), first(c), second(c)], axis=0)
                high, low = split(whole)
                there = pl.ds(pl.multiple_of(g * wide + i * 128, 128), 128)
                lhs[0:count, there] = high
                lhs[count : 2 * count, there] = low
                return 0

            lax.fori_loop(0, group // 2, assemble, 0)
        last = some[-1] + 1 == groups

        def one(n, _):
            there = pl.ds(pl.multiple_of(n * block, block), block)
            spectra = spec[:, there] if some[0] > 0 else None
            for g in some:
                a_h = ahi[group_planes(g), :, :, there].reshape(wide, block)
                a_l = alo[group_planes(g), :, :, there].reshape(wide, block)
                both = dot(lhs[:, g * wide : (g + 1) * wide], a_h)
                new = both[:count] + both[count:] + dot(lhs[0:count, g * wide : (g + 1) * wide], a_l)
                spectra = new if spectra is None else spectra + new
            if last:
                weights = kern[:, k * span : (k + 1) * span, there]
                part[k, :, there] = jnp.sum(weights * spectra.reshape(layers, span, block), axis=0)
            else:
                spec[:, there] = spectra
            return 0

        lax.fori_loop(0, blocks, one, 0)
        if last:
            for i in range(1, ny):
                r_copy(k, i).start()

    def times_matrix(n):
        there = pl.ds(pl.multiple_of(n * block, block), block)
        a_h = ahi[:, :, :, there].reshape(size, block)
        a_l = alo[:, :, :, there].reshape(size, block)
        both = dot(lhs[...], a_h)
        return both[:count] + both[count:] + dot(lhs[0:count, :], a_l)

    def r_copy(k, i):
        to = (y + i) % ny
        return pltpu.make_async_remote_copy(
            src_ref=part.at[k, pl.ds(pl.multiple_of(to * quarter, quarter), quarter)], dst_ref=rrecv.at[k, i],
            send_sem=rs_sem.at[k, i], recv_sem=rr_sem.at[k, i],
            device_id={"depth": y_peer(i)}, device_id_type=MESH)

    def z_copy(k):
        return pltpu.make_async_remote_copy(
            src_ref=rsum.at[k], dst_ref=zrecv.at[k], send_sem=z_sem.at[0, k], recv_sem=z_sem.at[1, k],
            device_id={"depth": sibling}, device_id_type=MESH)

    mine = pl.ds(pl.multiple_of(y * quarter, quarter), quarter)

    def m_copy(k, i):
        return pltpu.make_async_remote_copy(
            src_ref=misfit.at[k, mine], dst_ref=misfit.at[k, mine],
            send_sem=ms_sem.at[k, i], recv_sem=mr_sem.at[k, i],
            device_id={"depth": y_peer(i)}, device_id_type=MESH)

    def m_arrival(k, i):
        theirs = pl.ds(pl.multiple_of(((y + ny - i) % ny) * quarter, quarter), quarter)
        return pltpu.make_async_remote_copy(
            src_ref=misfit.at[k, mine], dst_ref=misfit.at[k, theirs],
            send_sem=ms_sem.at[k, i], recv_sem=mr_sem.at[k, i],
            device_id={"depth": y_peer(i)}, device_id_type=MESH)

    def reduce_rows(k):
        total = part[k, mine, :]
        for i in range(1, ny):
            r_copy(k, i).wait_recv()
            total = total + rrecv[k, i]
        rsum[k] = total
        z_copy(k).start()

    def spread(k):
        z_copy(k).wait_recv()
        first = k * span + y * quarter
        summed = rsum[k] + zrecv[k]
        values = summed - data[pl.ds(pl.multiple_of(first, quarter), quarter), :]
        freq_col = me * rows + first + lax.broadcasted_iota(jnp.int32, (quarter, size), 0)
        freq_row = lax.broadcasted_iota(jnp.int32, (quarter, size), 1)
        misfit[k, mine, :] = jnp.where((freq_col == 0) & (freq_row == 0), 0.0, values)
        for i in range(1, ny):
            m_copy(k, i).start()

    def weigh_misfit(k):
        for i in range(1, ny):
            m_arrival(k, i).wait_recv()

        def load(n, _):
            there = pl.ds(pl.multiple_of(n * block, block), block)
            weighted = kern[:, k * span : (k + 1) * span, there] * misfit[k, :, there][None]
            high, low = split(weighted.reshape(count, block))
            lhs[0:count, there] = high
            lhs[count : 2 * count, there] = low
            return 0

        lax.fori_loop(0, blocks, load, 0)

    left_all = lax.broadcasted_iota(jnp.int32, (layers, half, 128), 2) < 64

    def rows_out(k, begin, end):
        def one(i, _):
            n = (home * (group // per_block) + i) % blocks
            values = times_matrix(n)
            for s in range(block // 128):
                slab = values[:, s * 128 : (s + 1) * 128].reshape(layers, 2, half, 128)
                top, low = slab[:, 0], slab[:, 1]
                even = jnp.where(left_all, top, pltpu.roll(low, 64, 2))
                odd = jnp.where(left_all, pltpu.roll(top, 64, 2), low)
                bsend[k, n * per_block + 2 * s] = even.reshape(layers * half, 128)
                bsend[k, n * per_block + 2 * s + 1] = odd.reshape(layers * half, 128)

            @pl.when(i % (group // per_block) == group // per_block - 1)
            def _():
                g = i // (group // per_block)
                b_start(k, jnp.maximum(g * group, 1), (g + 1) * group)

            return 0

        lax.fori_loop(begin, end, one, 0)
        if begin == 0:
            brecv[k, me] = bsend[k, me]

    high_rows = layers * rows
    tile_rows = group * half

    def columns_back(k, some):
        for g in some:
            sources(g, b_arrival, k)
            for l in range(layers):
                tile = brecv[k, group_planes(g), l * half : (l + 1) * half, :].reshape(tile_rows, 128).T
                high, low = split(tile)
                for h in range(2):
                    there = pl.ds((2 * g + h) * tile_rows, tile_rows)
                    xt[l * rows : (l + 1) * rows, there] = high[h * 64 : (h + 1) * 64]
                    xt[high_rows + l * rows : high_rows + (l + 1) * rows, there] = low[h * 64 : (h + 1) * 64]
        first = k == 0 and some[0] == 0

        def one(n, _):
            there = pl.ds(pl.multiple_of(n * block, block), block)
            total = None if first else acc[:, there]
            for g in some:
                a_h = jnp.concatenate([ahi[group_planes(g), 2 * k + h, :, there].reshape(tile_rows, block) for h in range(2)], axis=0)
                a_l = jnp.concatenate([alo[group_planes(g), 2 * k + h, :, there].reshape(tile_rows, block) for h in range(2)], axis=0)
                where = pl.ds(2 * g * tile_rows, 2 * tile_rows)
                both = dot(xt[:, where], a_h)
                new = both[:high_rows] + both[high_rows:] + dot(xt[0:high_rows, where], a_l)
                total = new if total is None else total + new
            acc[:, there] = total
            return 0

        lax.fori_loop(0, blocks, one, 0)

    prow_copy = pltpu.make_async_remote_copy(
        src_ref=psend, dst_ref=precv, send_sem=h_sem.at[4], recv_sem=h_sem.at[5],
        device_id={"plane": after}, device_id_type=MESH)
    part_rows = rows // 2
    player_copies = [
        pltpu.make_async_remote_copy(
            src_ref=dual.at[2, layers - 1, pl.ds(h * part_rows, part_rows)],
            dst_ref=layer_prev.at[pl.ds(h * part_rows, part_rows)],
            send_sem=h_sem.at[6 + 2 * h], recv_sem=h_sem.at[7 + 2 * h],
            device_id={"depth": above}, device_id_type=MESH)
        for h in range(2)
    ]

    row8 = lax.broadcasted_iota(jnp.int32, (8, size), 0)
    col8 = lax.broadcasted_iota(jnp.int32, (8, size), 1)

    def update_dual():
        loads[1].wait()
        row_copy.wait()
        layer_copy.wait()
        for l in range(layers):
            vel[l, rows : rows + 1, :] = hrecv[l : l + 1, :]

        for l in range(layers):
            def dual_rows(i, _, l=l):
                off = pl.multiple_of(i * 8, 8)
                here = pl.ds(off, 8)
                v = vel[l, here, :]
                following = vel[l, pl.ds(pl.multiple_of(off + 8, 8), 8), :][0:1]
                next_row = jnp.where(row8 == 7, following, pltpu.roll(v, 7, 0))
                next_col = pltpu.roll(v, size - 1, 1)
                next_layer = vel[l + 1, here, :] if l + 1 < layers else layer_next[here, :]
                last_row = (me * rows + off + row8) == size - 1
                q0 = jnp.where(last_row, 0.0, dual[0, l, here, :] + dual_step * (next_row - v))
                q1 = jnp.where(col8 == size - 1, 0.0, dual[1, l, here, :] + dual_step * (next_col - v))
                q2 = dual[2, l, here, :] + dual_step * (next_layer - v)
                if l + 1 == layers:
                    q2 = jnp.where(my_depth == depths - 1, 0.0, q2)
                scale = lax.rsqrt(jnp.maximum(1.0, (q0 * q0 + q1 * q1 + q2 * q2) * (1.0 / (tv_weight * tv_weight))))
                dual[0, l, here, :] = q0 * scale
                dual[1, l, here, :] = q1 * scale
                dual[2, l, here, :] = q2 * scale
                return 0

            lax.fori_loop(0, rows // 8, dual_rows, 0)
        for l in range(layers):
            psend[l : l + 1, :] = dual[0, l, rows - 1 : rows, :]
        for l in range(layers, 8):
            psend[l : l + 1, :] = jnp.zeros((1, size), f32)
    def diverge(some, begin, end):
        for l in some:
            def div_rows(i, _, l=l):
                off = pl.multiple_of(i * 8, 8)
                here = pl.ds(off, 8)
                previous = dual[0, l, pl.ds(pl.multiple_of(jnp.maximum(off - 8, 0), 8), 8), :][7:8]
                outer = jnp.where(me == 0, 0.0, precv[l : l + 1, :])
                leading = jnp.where(i == 0, outer, previous)
                p0, p1, p2 = dual[0, l, here, :], dual[1, l, here, :], dual[2, l, here, :]
                prev_row = jnp.where(row8 == 0, leading, pltpu.roll(p0, 1, 0))
                prev_col = jnp.where(col8 == 0, 0.0, pltpu.roll(p1, 1, 1))
                if l > 0:
                    prev_layer = dual[2, l - 1, here, :]
                else:
                    prev_layer = jnp.where(my_depth == 0, 0.0, layer_prev[here, :])
                divergence = (p0 - prev_row) + (p1 - prev_col) + (p2 - prev_layer)
                v = vel[l, here, :]
                base[l, here, :] = v + primal_step * divergence
                root = lax.rsqrt(v)
                vel[l, here, :] = (primal_step * 0.25 * gardner_coef) * (root * jnp.sqrt(root))
                return 0

            lax.fori_loop(begin, end, div_rows, 0)

    early, late = tuple(range(groups - 1)), (groups - 1,)
    def update_velocity(some, begin, end):
        for l in some:
            def new_rows(i, _, l=l):
                here = pl.ds(pl.multiple_of(i * 8, 8), 8)
                there = pl.ds(pl.multiple_of(l * rows + i * 8, 8), 8)
                update = base[l, here, :] - vel[l, here, :] * acc[there, :]
                base[l, here, :] = jnp.clip(update, speed_floor, speed_ceiling)
                return 0

            lax.fori_loop(begin, end, new_rows, 0)

    rows_in(0, early, tuple(range(groups - 1)))
    rows_in(0, late, (None,) * (groups - 1) + (groups - 1,))
    reduce_rows(0)
    layer_copy.start()
    rows_in(1, early)
    spread(0)
    rows_in(1, late)
    weigh_misfit(0)
    reduce_rows(1)
    rows_out(0, 0, blocks)
    spread(1)
    update_dual()
    prow_copy.start()
    weigh_misfit(1)
    rows_out(1, 0, blocks)
    player_copies[0].start()
    player_copies[1].start()
    columns_back(0, early + late)
    prow_copy.wait()
    diverge(range(1, layers), 0, rows // 8)
    columns_back(1, early)
    columns_back(1, late)
    update_velocity(range(1, layers), 0, rows // 8)
    player_copies[0].wait()
    diverge((0,), 0, rows // 16)
    update_velocity((0,), 0, rows // 16)
    player_copies[1].wait()
    diverge((0,), rows // 16, rows // 8)
    update_velocity((0,), rows // 16, rows // 8)

    def ended(t, _):
        g_copy(0, t, me).wait_send()
        g_copy(1, t, me).wait_send()
        b_copy(0, t, me).wait_send()
        b_copy(1, t, me).wait_send()
        return 0

    lax.fori_loop(1, planes, ended, 0)
    for k in range(chunks):
        z_copy(k).wait_send()
        for i in range(1, ny):
            r_copy(k, i).wait_send()
            m_copy(k, i).wait_send()


def store_kernel(vel, dual, vel_out, dual_out, sem):
    layers = vel.shape[0]
    copies = [
        pltpu.make_async_copy(dual.at[c, l], dual_out.at[c, l], sem.at[c, l]) for c in range(3) for l in range(layers)
    ]
    copies += [pltpu.make_async_copy(vel.at[l], vel_out.at[l], sem.at[3, l]) for l in range(layers)]
    for copy in copies:
        copy.start()
    for copy in copies:
        copy.wait()


def body(velocity, dual_field, kernel, data_spec, high, low):
    planes = lax.axis_size("plane")
    depths = lax.axis_size("depth")
    layers, rows, size = velocity.shape
    span = rows // chunks
    half = span // 2
    ny = depths // 2
    quarter = span // ny
    hbm = pl.BlockSpec(memory_space=pltpu.HBM)
    vmem = pltpu.VMEM
    dma = pltpu.SemaphoreType.DMA
    scratch = [
        vmem((layers, rows + 8, size), f32),
        vmem((layers, rows, size), f32),
        vmem((rows, size), f32),
        vmem((planes, 2 * chunks, half, size), bf16),
        vmem((planes, 2 * chunks, half, size), bf16),
        vmem((size, 256), bf16),
        vmem((size, 256), bf16),
        vmem((size, 256), bf16),
        vmem((size, 256), bf16),
        vmem((chunks, planes, half, 384), f32),
        vmem((chunks, planes, half, 384), f32),
        vmem((chunks, planes, layers * half, 128), f32),
        vmem((chunks, planes, layers * half, 128), f32),
        vmem((2 * layers * span, size), bf16),
        vmem((chunks, span, size), f32),
        vmem((chunks, quarter, size), f32),
        vmem((chunks, ny, quarter, size), f32),
        vmem((chunks, quarter, size), f32),
        vmem((chunks, span, size), f32),
        vmem((2 * layers * rows, 2 * planes * half), bf16),
        vmem((layers * rows, size), f32),
        vmem((layers * span, size), f32),
        vmem((8, size), f32),
        vmem((8, size), f32),
        vmem((8, size), f32),
        vmem((8, size), f32),
        vmem((rows, size), f32),
        vmem((rows, size), f32),
        dma((4,)),
        dma((2, 2 * chunks)),
        dma((chunks, planes)),
        dma((chunks, planes)),
        dma((chunks, planes)),
        dma((chunks, planes)),
        dma((chunks, ny)),
        dma((chunks, ny)),
        dma((2, chunks)),
        dma((chunks, ny)),
        dma((chunks, ny)),
        dma((10,)),
    ]
    on_chip = pl.BlockSpec(memory_space=vmem)
    updated = pl.pallas_call(
        functools.partial(step_kernel, planes, depths, size, layers),
        out_shape=(vmem(velocity.shape, f32), vmem(dual_field.shape, f32)),
        in_specs=[hbm] * 6,
        out_specs=(on_chip, on_chip),
        scratch_shapes=scratch,
        compiler_params=pltpu.CompilerParams(
            collective_id=0, has_side_effects=True, vmem_limit_bytes=48 * 1024 * 1024
        ),
        cost_estimate=pl.CostEstimate(
            flops=24 * layers * rows * size * size, bytes_accessed=60 * layers * rows * size, transcendentals=layers * rows * size
        ),
    )(velocity, dual_field, kernel, data_spec, high, low)
    return pl.pallas_call(
        store_kernel,
        out_shape=(
            jax.ShapeDtypeStruct(velocity.shape, f32),
            jax.ShapeDtypeStruct(dual_field.shape, f32),
        ),
        in_specs=[on_chip, on_chip],
        out_specs=(hbm, hbm),
        scratch_shapes=[dma((4, layers))],
        compiler_params=pltpu.CompilerParams(has_side_effects=True, vmem_limit_bytes=8 * 1024 * 1024),
    )(*updated)


def solution(mesh):
    in_specs = (
        P("depth", "plane", None),
        P(None, "depth", "plane", None),
        P("depth", "plane", None),
        P("plane", None),
        P(),
        P(),
    )
    out_specs = (P("depth", "plane", None), P(None, "depth", "plane", None))
    mapped = jax.shard_map(body, mesh=mesh, in_specs=in_specs, out_specs=out_specs, check_vma=False)

    def run(velocity, dual_field, kernel, data_spec):
        size, planes = velocity.shape[-1], mesh.shape["plane"]
        shape = (planes, 2 * chunks, size // planes // (2 * chunks), size)
        high, low = (part.reshape(shape) for part in cas_parts(size))
        return mapped(velocity, dual_field, kernel, data_spec, jnp.asarray(high), jnp.asarray(low))

    return run
```
